32 devices in a mesh: rel: 8 (over z, y), dom: 4 (over x, core).
Axes of the slice: x: 2, y: 2, z: 4, core: 2. Of those that a mesh axis runs over, the one named last changes fastest.
Arguments:
- edge_feats: bfloat16 [4, 4096, 1024], P('dom', 'rel'), may hold values from -6 to 6
- gain: float32 [1024], replicated, may hold values from 0.25 to 1.75
- w_in: bfloat16 [8, 1024, 2048], P('rel'), may hold values from -0.1875 to 0.1875
- w_out: bfloat16 [8, 2048, 1024], P('rel'), may hold values from -0.125 to 0.125
- rel_type: int32 [4, 4096, 1], P('dom', 'rel'), may hold values from 0 to 7; in each aligned block of 512 rows (0 to 511, 512 to 1023, ..., all dimensions but the last counted through in order) at most 128 rows name the same one
- dst_node: int32 [4, 4096], P('dom', 'rel'), may hold values from 0 to 1023, as said below
Outputs:
- node_state: float32 [4, 256, 1024], P('dom', 'rel')
The draws below stay inside these ranges and needn't reach their ends.
Inputs may be any that keep to these rules, and one draw needn't show every extreme that they name: `rel_type`: in the 512 edges of one device (aligned blocks of rows) at most 128 edges have one relation type, and some relation has exactly 128 there; every relation occurs. `dst_node`: node ids; node n belongs to partition group n // 256 and, within it, to owner index (n // 32) % 8. In the 512 edges of one device (aligned blocks of rows) at most 32 point to nodes of one (group, owner index) pair, and some pair has exactly 32 there.
All inputs are finite; a program needn't handle non-finite values.
Results may differ from the reference program's by a relative error of at most 0.011.
Values may be sent and summed in bfloat16 or wider, within the bound.
No kernel may reach another device: no remote copies, remote signals or barrier semaphores. Data moves between devices by JAX's collectives and lax.ppermute only.
A program may use at most 128 MiB of HBM per device.

```python
import math
import jax
import jax.numpy as jnp
import numpy as np
from jax import lax

D = 1024
HID = 2048
E_DEV = 512
NODE_DEV = 32
RELS = 8
GROUPS = 4
CAP = 128
ROUTE_CAP = 32
EDGES_GRP = 4096
NODE_GRP = 256
NODES = 1024


def draw_dst_node(key, part):
    dev_count = RELS * GROUPS
    device_keys = jax.random.split(jax.random.fold_in(key, 7), dev_count)

    def one_device(device_key):
        key_full, key_rest, key_order, key_within = jax.random.split(device_key, 4)
        busiest = jax.random.randint(key_full, (), 0, dev_count, dtype=jnp.int32)
        others = jnp.arange((dev_count - 1) * ROUTE_CAP, dtype=jnp.int32) // ROUTE_CAP
        others = others + (others >= busiest).astype(jnp.int32)
        others = jax.random.permutation(key_rest, others)[:E_DEV - ROUTE_CAP]
        owners = jnp.concatenate([jnp.full((ROUTE_CAP,), busiest, jnp.int32), others])
        owners = jax.random.permutation(key_order, owners)
        within = jax.random.randint(key_within, (E_DEV,), 0, NODE_DEV, dtype=jnp.int32)
        return (owners % GROUPS * NODE_GRP + owners // GROUPS * NODE_DEV + within).astype(jnp.int32)
    return jax.vmap(one_device)(device_keys).reshape(GROUPS, EDGES_GRP)


def shard_levels(rng, extent, pieces, smallest, top_value):
    factor_of, own = 1.0, jax.random.fold_in(rng, 6)
    for axis_at, parts in pieces:
        steps = jnp.exp(jax.random.uniform(jax.random.fold_in(own, axis_at), (parts,), jnp.float32, smallest / len(pieces), top_value / len(pieces)))
        factor_of = factor_of * jnp.repeat(steps, extent[axis_at] // parts).reshape([-1 if axis == axis_at else 1 for axis in range(len(extent))])
    return factor_of


def routed_block(key, own, number, rows, number_of, top, most, skew):
    sequence = jax.random.permutation(key, number_of)
    packed, usual = shares(number_of, rows * top, most, skew, True), shares(number_of, rows * top, most, skew, False)
    places = jnp.arange(number_of)

    def named(tallies, rotation):
        used = int((tallies > 0).sum())
        fixed = max(1, used // 4)
        shifted = fixed + (places - fixed + rotation * (used - fixed)) % max(1, number_of - fixed)
        return jnp.zeros((number_of,), jnp.int32).at[sequence[jnp.where(places < fixed, places, shifted)]].set(jnp.asarray(tallies, jnp.int32))

    tallies = jnp.where(number % 4 == 0, named(packed, number // 4), named(usual, number - number // 4 - 1))
    mixed = jax.random.permutation(jax.random.fold_in(own, 3), number_of)
    source_of, taker = mixed[0:number_of // 2 * 2:2], mixed[1:number_of // 2 * 2:2]
    margin = jnp.minimum(tallies[source_of] - 1, most - tallies[taker]) // 2
    margin = jnp.where((source_of == sequence[0]) | (taker == sequence[0]) | (tallies[taker] == 0), 0, jnp.maximum(margin, 0))
    shifted = jax.random.randint(jax.random.fold_in(own, 4), (number_of // 2,), 0, 1 << 20) % (margin + 1)
    tallies = tallies.at[source_of].add(-shifted).at[taker].add(shifted)
    labels = jnp.searchsorted(jnp.cumsum(tallies), jnp.arange(rows * top), side="right").astype(jnp.int32)
    grid = labels.reshape(top, rows).T
    grid = grid[jax.random.permutation(jax.random.fold_in(own, 1), rows)]
    rotation = jax.random.randint(jax.random.fold_in(own, 2), (rows, 1), 0, top)
    return jnp.take_along_axis(grid, (jnp.arange(top)[None, :] + rotation) % top, axis=1)


def shares(amount, total, limit, skew, full):
    weights = [(1 << 20) // math.isqrt(grade ** skew) + 1 for grade in range(1, amount + 1)]
    largest = limit if full else min(limit, max(-(-total // amount), total * weights[0] // sum(weights)))
    least = 1 if total - largest >= amount - 1 else 0
    counts, spare = [largest] + [least] * (amount - 1), total - largest - least * (amount - 1)
    while spare > 0:
        free = [i for i in range(1, amount) if counts[i] < largest] or [i for i in range(1, amount) if counts[i] < limit]
        pool, budget = sum([weights[i] for i in free]), spare
        for i in free:
            more = min(limit - counts[i], max(1, budget * weights[i] // pool), spare)
            counts[i] = counts[i] + more
            spare = spare - more
    return np.array(counts)


def bell_draw(rng, shape, width, reach, cuts=(), held_as=jnp.bfloat16):
    drawn = width * jax.random.normal(rng, shape, jnp.float32)
    if cuts:
        drawn = drawn * shard_levels(rng, shape, cuts, -0.22, 0.18)
    return jnp.clip(drawn, -reach, reach).astype(held_as)


def setup_inputs(seed: int = 0) -> dict:
    key_list = jax.random.split(jax.random.key(seed), 7)
    edge_feats = bell_draw(key_list[0], (GROUPS, EDGES_GRP, D), 1.0, 6.0, ((0, 4), (1, 8)))
    gain = jnp.clip(1.0 + 0.15 * jax.random.normal(key_list[1], (D,), jnp.float32), 0.25, 1.75)
    w_in = bell_draw(key_list[2], (RELS, D, HID), D ** -0.5, 0.1875, ((0, 8),))
    w_out = bell_draw(key_list[3], (RELS, HID, D), HID ** -0.5, 0.125, ((0, 8),))
    rel_type_keys = jax.random.split(jax.random.fold_in(key_list[4], 1), GROUPS * EDGES_GRP // E_DEV)
    rel_type_turns = jax.random.permutation(jax.random.fold_in(key_list[4], 3), GROUPS * EDGES_GRP // E_DEV)
    rel_type = jax.vmap(lambda own, number: routed_block(jax.random.fold_in(key_list[4], 2), own, number, E_DEV, RELS, 1, CAP, 2))(rel_type_keys, rel_type_turns).reshape((GROUPS, EDGES_GRP, 1))
    dst_node = draw_dst_node(jax.random.fold_in(key_list[6], 71), 0)
    return {"edge_feats": edge_feats, "gain": gain, "w_in": w_in, "w_out": w_out, "rel_type": rel_type, "dst_node": dst_node}


def reference(edge_feats, gain, w_in, w_out, rel_type, dst_node):
    feats = edge_feats.reshape(-1, D).astype(jnp.float32)
    scale_rows = lax.rsqrt(lax.optimization_barrier(jnp.mean(feats * feats, axis=1, keepdims=True)) + 1e-06)
    normed = (feats * scale_rows * gain.astype(jnp.float32)[None, :]).astype(jnp.bfloat16)
    kinds = rel_type.reshape(-1).astype(jnp.int32)
    targets = dst_node.reshape(-1).astype(jnp.int32)
    padded = 2 * GROUPS * E_DEV

    def one_relation(carry, index):
        order = jnp.argsort((kinds != index).astype(jnp.int32), stable=True)[:padded]
        live = kinds[order] == index
        picked = normed[order]
        hidden = jax.nn.gelu(jnp.dot(picked, w_in[index], preferred_element_type=jnp.float32), approximate=False).astype(jnp.bfloat16)
        message = jnp.dot(hidden, w_out[index], preferred_element_type=jnp.float32).astype(jnp.bfloat16)
        chosen = jnp.where(live, targets[order], NODES).astype(jnp.int32)
        summed = jax.ops.segment_sum(message.astype(jnp.float32), chosen, num_segments=NODES + 1)
        return (carry + summed[:NODES], None)
    sums, _ = lax.scan(one_relation, jnp.zeros((NODES, D), jnp.float32), jnp.arange(RELS, dtype=jnp.int32))
    node_state = sums * (1.0 / math.sqrt(E_DEV / NODE_DEV))
    return node_state.reshape(GROUPS, NODE_GRP, D)
```

```python
import functools
import math

import jax
import jax.numpy as jnp
from jax import lax
from jax.experimental import pallas as pl
from jax.experimental.pallas import tpu as pltpu
from jax.sharding import PartitionSpec as P

NODE_DEV = 32
VMEM_BYTES = 48 * 1024 * 1024
VM = pl.BlockSpec(memory_space=pltpu.VMEM)
SM = pl.BlockSpec(memory_space=pltpu.SMEM)


def pack_kernel(relations, slots, place_ref, kinds_ref, dest_ref, feats_ref, gain_ref, *outs):
    blocks, ids_ref, normed_ref = outs[:relations], outs[relations], outs[relations + 1]
    rows, width = feats_ref.shape
    part = 128
    gain = gain_ref[...]

    def norm(i, carry):
        at = pl.ds(pl.multiple_of(i * part, part), part)
        feats = feats_ref[at, :].astype(jnp.float32)
        scale = lax.rsqrt(jnp.mean(feats * feats, axis=1, keepdims=True) + 1e-06)
        normed_ref[at, :] = (feats * scale * gain).astype(jnp.bfloat16)
        return carry

    lax.fori_loop(0, rows // part, norm, 0)
    offset = kinds_ref[...] ^ place_ref[0]
    lanes = max(relations, 16)
    marks = offset == lax.broadcasted_iota(jnp.int32, (lanes, rows), 0)
    ones = marks.astype(jnp.bfloat16)
    before = (
        lax.broadcasted_iota(jnp.int32, (rows, rows), 0) < lax.broadcasted_iota(jnp.int32, (rows, rows), 1)
    ).astype(jnp.bfloat16)
    count = jnp.dot(ones, before, preferred_element_type=jnp.float32)
    rank = jnp.sum(jnp.where(marks, count, 0.0), axis=0, keepdims=True).astype(jnp.int32)
    slot = offset * slots + rank
    dest = dest_ref[...]
    line = lax.broadcasted_iota(jnp.int32, (16, rows), 0)
    coded = jnp.where(
        line == 0, dest // NODE_DEV, jnp.where(line == 1, dest % NODE_DEV, jnp.where(line == 2, 1, 0))
    ).astype(jnp.bfloat16)
    normed = normed_ref[...]
    for d in range(relations):
        pick = (slot == lax.broadcasted_iota(jnp.int32, (slots, rows), 0) + d * slots).astype(jnp.bfloat16)
        blocks[d][...] = jnp.dot(pick, normed, preferred_element_type=jnp.float32).astype(jnp.bfloat16)
        got = lax.dot_general(
            coded, pick, (((1,), (1,)), ((), ())), preferred_element_type=jnp.float32
        ).astype(jnp.int32)
        ids_ref[d : d + 1, :] = jnp.where(got[2:3] > 0, got[0:1] * NODE_DEV + got[1:2], -1)


def pack(place, kinds, dest, feats, gain, relations, slots):
    rows, width = feats.shape
    shapes = [jax.ShapeDtypeStruct((slots, width), jnp.bfloat16)] * relations
    shapes.append(jax.ShapeDtypeStruct((relations, slots), jnp.int32))
    outs = pl.pallas_call(
        functools.partial(pack_kernel, relations, slots),
        out_shape=shapes,
        in_specs=[SM, VM, VM, VM, VM],
        out_specs=[VM] * len(shapes),
        scratch_shapes=[pltpu.VMEM((rows, width), jnp.bfloat16)],
        compiler_params=pltpu.CompilerParams(vmem_limit_bytes=24 * 1024 * 1024),
        cost_estimate=pl.CostEstimate(
            flops=2 * rows * width * relations * slots, bytes_accessed=4 * rows * width * 2, transcendentals=0
        ),
        name="pack",
    )(place, kinds, dest, feats, gain)
    return outs[:relations], outs[relations]


def gelu(x):
    return 0.5 * x * (1.0 + lax.erf(x * math.sqrt(0.5)))


def expert_kernel(first, count, slots, groups, relations, has_sums, last, place_ref, ids_ref, *refs):
    blocks, refs = refs[:count], refs[count:]
    w_first_ref, w_second_ref, refs = refs[0], refs[1], refs[2:]
    if has_sums:
        sums_ref, refs = refs[0], refs[1:]
    outs, (x_ref, hidden_ref, row_ref) = refs[:-3], refs[-3:]
    width, inner = w_first_ref.shape
    rows = count * slots
    mine, base = place_ref[0], place_ref[1]
    half = relations // 2
    for i in range(count):
        x_ref[i * slots : (i + 1) * slots, :] = blocks[i][...]
        node = ids_ref[mine ^ (first + i), first + i : first + i + 1, :]
        away = node ^ base
        j = away % NODE_DEV
        y = (away // NODE_DEV) % 2
        z = (away // (2 * NODE_DEV)) % half
        g = away // (NODE_DEV * relations)
        at = (((g % 2) * 2 + g // 2) * 2 + y) * half * NODE_DEV + z * NODE_DEV + j
        row_ref[:, i * slots : (i + 1) * slots] = jnp.where(node < 0, -1, at)
    part = 256

    def up(i, carry):
        at = pl.ds(pl.multiple_of(i * part, part), part)
        h = jnp.dot(x_ref[...], w_first_ref[:, at], preferred_element_type=jnp.float32)
        hidden_ref[:, at] = gelu(h).astype(jnp.bfloat16)
        return carry

    lax.fori_loop(0, inner // part, up, 0, unroll=2)
    nodes = groups * relations * NODE_DEV
    piece = nodes // 8

    def down(i, carry):
        at = pl.ds(pl.multiple_of(i * part, part), part)
        message = jnp.dot(hidden_ref[...], w_second_ref[:, at], preferred_element_type=jnp.float32)
        message = message.astype(jnp.bfloat16)
        for b in range(8):
            table = (
                row_ref[...] == lax.broadcasted_iota(jnp.int32, (piece, rows), 0) + b * piece
            ).astype(jnp.bfloat16)
            total = jnp.dot(table, message, preferred_element_type=jnp.float32)
            if has_sums:
                total = total + sums_ref[b * piece : (b + 1) * piece, at]
            if last:
                outs[b][:, at] = total.astype(jnp.bfloat16)
            else:
                outs[0][b * piece : (b + 1) * piece, at] = total
        return carry

    lax.fori_loop(0, width // part, down, 0)


def expert(place, ids, blocks, first, w_first, w_second, sums, groups, relations, last):
    count = len(blocks)
    slots, width = blocks[0].shape
    inner = w_first.shape[1]
    rows = count * slots
    nodes = groups * relations * NODE_DEV
    if last:
        shapes = [jax.ShapeDtypeStruct((nodes // 8, width), jnp.bfloat16)] * 8
    else:
        shapes = [jax.ShapeDtypeStruct((nodes, width), jnp.float32)]
    args = [place, ids, *blocks, w_first, w_second] + ([] if sums is None else [sums])
    return pl.pallas_call(
        functools.partial(
            expert_kernel, first, count, slots, groups, relations, sums is not None, last
        ),
        out_shape=shapes,
        in_specs=[SM] + [VM] * (len(args) - 1),
        out_specs=[VM] * len(shapes),
        scratch_shapes=[
            pltpu.VMEM((rows, width), jnp.bfloat16),
            pltpu.VMEM((rows, inner), jnp.bfloat16),
            pltpu.VMEM((1, rows), jnp.int32),
        ],
        compiler_params=pltpu.CompilerParams(vmem_limit_bytes=VMEM_BYTES),
        cost_estimate=pl.CostEstimate(
            flops=4 * rows * width * inner + 2 * nodes * rows * width,
            bytes_accessed=4 * width * inner + 2 * rows * width + 4 * nodes * width,
            transcendentals=rows * inner,
        ),
        name="expert",
    )(*args)


def local(edge_feats, gain, w_in, w_out, rel_type, dst_node):
    rows = edge_feats.shape[1]
    relations = lax.axis_size("rel")
    groups = lax.axis_size("dom")
    slots = 2 * rows // relations
    half = relations // 2
    mine = lax.axis_index("rel")
    place = jnp.stack([mine, (lax.axis_index("dom") * relations + mine) * NODE_DEV]).astype(jnp.int32)
    blocks, ids = pack(
        place, rel_type.reshape(1, rows), dst_node, edge_feats[0], gain[None, :], relations, slots
    )
    ids = lax.all_gather(ids, "rel")

    def swap(value, d):
        return lax.ppermute(value, "rel", [(i, i ^ d) for i in range(relations)])

    order = list(range(half, relations)) + list(range(1, half))
    held = {0: blocks[0]}
    for d in order:
        held[d] = swap(blocks[d], d)
    cuts = [0, half, half + relations // 4, relations]
    sums = None
    for k in range(3):
        sums = expert(
            place, ids, [held[d] for d in range(cuts[k], cuts[k + 1])], cuts[k], w_in[0], w_out[0],
            None if sums is None else sums[0], groups, relations, k == 2,
        )

    def move(value, dom_bits, rel_bits):
        pairs = [
            (r * groups + g, (r ^ rel_bits) * groups + (g ^ dom_bits))
            for g in range(groups) for r in range(relations)
        ]
        return lax.ppermute(value, ("rel", "dom"), pairs)

    f32, bf16 = jnp.float32, jnp.bfloat16
    sums = [
        sums[b].astype(f32) + move(sums[4 + b], 1, 0).astype(f32) for b in range(4)
    ]
    total = sums[0]
    for b in (1, 2, 3):
        total = total + move(sums[b].astype(bf16), 2 * (b // 2), b % 2).astype(f32)
    total = total.reshape(half, NODE_DEV, -1)
    state = total[0]
    for z in range(1, half):
        state = state + move(total[z].astype(bf16), 0, 2 * z).astype(f32)
    return (state * (1.0 / math.sqrt(rows / NODE_DEV)))[None]


def solution(mesh):
    in_specs = (
        P("dom", "rel", None),
        P(),
        P("rel", None, None),
        P("rel", None, None),
        P("dom", "rel", None),
        P("dom", "rel"),
    )
    out_specs = P("dom", "rel", None)
    return jax.shard_map(local, mesh=mesh, in_specs=in_specs, out_specs=out_specs, check_vma=False)
```

```python
import functools
import math

import jax
import jax.numpy as jnp
from jax import lax
from jax.experimental import pallas as pl
from jax.experimental.pallas import tpu as pltpu
from jax.sharding import PartitionSpec as P

NODE_DEV = 32
LANES = 128
EXTRA = 16
CUTS = (0.0, 1.0)
MIB = 1024 * 1024
VM = pl.BlockSpec(memory_space=pltpu.VMEM)
SM = pl.BlockSpec(memory_space=pltpu.SMEM)
HB = pl.BlockSpec(memory_space=pltpu.HBM)
F32 = jnp.float32
BF16 = jnp.bfloat16
I32 = jnp.int32


def write_blocks(first, slots, slot, coded, normed, blocks):
    rows, width = normed.shape
    for i, block in enumerate(blocks):
        at = lax.broadcasted_iota(I32, (slots, rows), 0) + (first + i) * slots
        pick = (slot == at).astype(BF16)
        picked = jnp.dot(pick, normed, preferred_element_type=F32).astype(BF16)
        for c in range(width // LANES):
            block[c * slots : (c + 1) * slots, :] = picked[:, c * LANES : (c + 1) * LANES]
        ids = lax.dot_general(coded, pick, (((1,), (1,)), ((), ())), preferred_element_type=F32)
        block[width // LANES * slots :, :slots] = ids.astype(BF16)


def pack_kernel(relations, slots, first, count, place_ref, kinds_hbm, dest_hbm, feats_hbm, gain_hbm, *refs):
    blocks, (normed_ref, slot_ref, coded_ref), scratch = (
        refs[:count], refs[count:-6], refs[-6:],
    )
    kinds_ref, dest_ref, gain_ref, feats_ref, sems, feat_sems = scratch
    rows, width = feats_ref.shape
    part = rows // 4
    small = [
        pltpu.make_async_copy(kinds_hbm, kinds_ref, sems.at[0]),
        pltpu.make_async_copy(dest_hbm, dest_ref, sems.at[1]),
        pltpu.make_async_copy(gain_hbm, gain_ref, sems.at[2]),
    ]
    large = [
        pltpu.make_async_copy(
            feats_hbm.at[pl.ds(i * part, part), :], feats_ref.at[pl.ds(i * part, part), :], feat_sems.at[i]
        )
        for i in range(4)
    ]
    for copy in small + large:
        copy.start()
    before = (
        lax.broadcasted_iota(I32, (rows, rows), 0) < lax.broadcasted_iota(I32, (rows, rows), 1)
    ).astype(BF16)
    for copy in small:
        copy.wait()
    offset = kinds_ref[...] ^ place_ref[0]
    marks = offset == lax.broadcasted_iota(I32, (max(relations, 16), rows), 0)
    count = jnp.dot(marks.astype(BF16), before, preferred_element_type=F32)
    rank = jnp.sum(jnp.where(marks, count, 0.0), axis=0, keepdims=True).astype(I32)
    slot = offset * slots + rank
    slot_ref[...] = slot
    dest = dest_ref[...]
    line = lax.broadcasted_iota(I32, (EXTRA, rows), 0)
    coded = jnp.where(
        line == 0, dest // NODE_DEV, jnp.where(line == 1, dest % NODE_DEV, jnp.where(line == 2, 1, 0))
    ).astype(BF16)
    coded_ref[...] = coded
    gain = gain_ref[...]
    for i in range(4):
        large[i].wait()
        at = slice(i * part, (i + 1) * part)
        feats = feats_ref[at, :].astype(F32)
        scale = lax.rsqrt(jnp.mean(feats * feats, axis=1, keepdims=True) + 1e-06)
        normed_ref[at, :] = (feats * scale * gain).astype(BF16)
    write_blocks(first, slots, slot, coded, normed_ref[...], blocks)


def pack_more_kernel(slots, first, count, normed_ref, slot_ref, coded_ref, *refs):
    write_blocks(first, slots, slot_ref[...], coded_ref[...], normed_ref[...], refs[-count:])


def pack_more(kept, first, count, slots, after=()):
    rows, width = kept[0].shape
    block = jax.ShapeDtypeStruct((width // LANES * slots + EXTRA, LANES), BF16)
    return pl.pallas_call(
        functools.partial(pack_more_kernel, slots, first, count),
        out_shape=[block] * count,
        in_specs=[VM] * 3 + [HB] * len(after),
        out_specs=[VM] * count,
        compiler_params=pltpu.CompilerParams(vmem_limit_bytes=16 * MIB),
        cost_estimate=pl.CostEstimate(flops=1, bytes_accessed=1, transcendentals=0),
        name="pack_more",
    )(*kept, *after)


def pack(place, kinds, dest, feats, gain, relations, slots, first, count):
    rows, width = feats.shape
    block = jax.ShapeDtypeStruct((width // LANES * slots + EXTRA, LANES), BF16)
    shapes = [block] * count + [
        jax.ShapeDtypeStruct((rows, width), BF16),
        jax.ShapeDtypeStruct((1, rows), I32),
        jax.ShapeDtypeStruct((EXTRA, rows), BF16),
    ]
    outs = pl.pallas_call(
        functools.partial(pack_kernel, relations, slots, first, count),
        out_shape=shapes,
        in_specs=[SM, HB, HB, HB, HB],
        out_specs=[VM] * len(shapes),
        scratch_shapes=[
            pltpu.VMEM((1, rows), I32),
            pltpu.VMEM((1, rows), I32),
            pltpu.VMEM((1, width), F32),
            pltpu.VMEM((rows, width), BF16),
            pltpu.SemaphoreType.DMA((3,)),
            pltpu.SemaphoreType.DMA((4,)),
        ],
        compiler_params=pltpu.CompilerParams(vmem_limit_bytes=16 * MIB),
        cost_estimate=pl.CostEstimate(flops=1, bytes_accessed=1, transcendentals=0),
        name="pack_far",
    )(place, *[pltpu.with_memory_space_constraint(a, pltpu.HBM) for a in (kinds, dest, feats, gain)])
    return outs[:count], outs[count:]


def gelu(x):
    return 0.5 * x * (1.0 + lax.erf(x * math.sqrt(0.5)))


def load_block(block_ref, x_ref, row, base, groups, relations):
    width = x_ref.shape[1]
    slots = (block_ref.shape[0] - EXTRA) * LANES // width
    for c in range(width // LANES):
        x_ref[row : row + slots, c * LANES : (c + 1) * LANES] = block_ref[c * slots : (c + 1) * slots, :]
    ids = block_ref[width // LANES * slots :, :slots].astype(F32).astype(I32)
    owner = ids[0:1] ^ base
    half = relations // 2
    y, z, g = owner % 2, owner // 2 % half, owner // relations
    at = ((((g % 2) * 2 + g // 2) * 2 + y) * half + z) * NODE_DEV + ids[1:2]
    return jnp.where(ids[2:3] > 0, at, -1)


def up(x_ref, w_first_ref, hidden_ref):
    inner = w_first_ref.shape[1]
    part = 256

    def step(i, carry):
        at = pl.ds(pl.multiple_of(i * part, part), part)
        h = jnp.dot(x_ref[...], w_first_ref[:, at], preferred_element_type=F32)
        hidden_ref[:, at] = gelu(h).astype(BF16)
        return carry

    lax.fori_loop(0, inner // part, step, 0, unroll=8)


def down(hidden_ref, w_second_ref, table_ref, sums_ref, outs, left, right):
    part = 256
    nodes = table_ref.shape[0]
    piece = nodes // len(outs)
    messages = [
        jnp.dot(
            hidden_ref[...], w_second_ref[:, start : min(start + part, right)], preferred_element_type=F32
        ).astype(BF16)
        for start in range(left, right, part)
    ]
    for i, message in enumerate(messages):
        start = left + i * part
        size = message.shape[1]
        total = jnp.dot(table_ref[...], message, preferred_element_type=F32)
        if sums_ref is not None:
            total = total + sums_ref[:, start : start + size]
        for b, out in enumerate(outs):
            out[:, start - left : start - left + size] = total[b * piece : (b + 1) * piece].astype(out.dtype)


def expert_kernel(count, slots, groups, relations, has_sums, right, place_ref, *refs):
    blocks, refs = refs[:count], refs[count:]
    w_first_ref, w_second_ref, refs = refs[0], refs[1], refs[2:]
    sums_ref = None
    if has_sums:
        sums_ref, refs = refs[0], refs[1:]
    outs, (token_ref, hidden_ref, table_ref, x_ref) = refs[:-4], refs[-4:]
    token_ref[...] = jnp.zeros_like(token_ref)
    nodes = table_ref.shape[0]
    for i in range(count):
        line = load_block(blocks[i], x_ref, i * slots, place_ref[1], groups, relations)
        table_ref[:, i * slots : (i + 1) * slots] = (
            line == lax.broadcasted_iota(I32, (nodes, slots), 0)
        ).astype(BF16)
    up(x_ref, w_first_ref, hidden_ref)
    down(hidden_ref, w_second_ref, table_ref, sums_ref, outs, 0, right)


def more_kernel(left, right, hidden_ref, table_ref, w_second_ref, sums_ref, *outs):
    down(hidden_ref, w_second_ref, table_ref, sums_ref, outs, left, right)


def expert(place, blocks, w_first, w_second, sums, groups, relations, edges):
    count = len(blocks)
    width, inner = w_first.shape
    slots = (blocks[0].shape[0] - EXTRA) * LANES // width
    rows = count * slots
    nodes = groups * relations * NODE_DEV
    if edges is None:
        right, shapes = width, [jax.ShapeDtypeStruct((nodes, width), F32)]
    else:
        right, shapes = edges[1], [jax.ShapeDtypeStruct((nodes // 8, edges[1]), BF16)] * 8
    shapes.append(jax.ShapeDtypeStruct((8, LANES), F32))
    kept = [jax.ShapeDtypeStruct((rows, inner), BF16), jax.ShapeDtypeStruct((nodes, rows), BF16)]
    scratch = [pltpu.VMEM(s.shape, s.dtype) for s in kept]
    args = [place, *blocks, w_first, w_second] + ([] if sums is None else [sums])
    keep = edges is not None
    params = pltpu.CompilerParams(vmem_limit_bytes=16 * MIB if relations <= 8 else 48 * MIB)
    outs = pl.pallas_call(
        functools.partial(expert_kernel, count, slots, groups, relations, sums is not None, right),
        out_shape=shapes + kept * keep,
        in_specs=[SM] + [VM] * (len(args) - 1),
        out_specs=[VM] * (len(shapes) + 2 * keep),
        scratch_shapes=scratch * (not keep) + [pltpu.VMEM((rows, width), BF16)],
        compiler_params=params,
        cost_estimate=pl.CostEstimate(flops=1, bytes_accessed=1, transcendentals=0),
        name="expert",
    )(*args)
    if edges is None:
        return outs
    pieces = [outs[:8]]
    for left, right in zip(edges[1:-1], edges[2:]):
        pieces.append(
            pl.pallas_call(
                functools.partial(more_kernel, left, right),
                out_shape=[jax.ShapeDtypeStruct((nodes // 8, right - left), BF16)] * 8,
                in_specs=[VM] * 4,
                out_specs=[VM] * 8,
                compiler_params=params,
                cost_estimate=pl.CostEstimate(flops=1, bytes_accessed=1, transcendentals=0),
                name="expert_more",
            )(outs[9], outs[10], w_second, sums)
        )
    return pieces


def local(edge_feats, gain, w_in, w_out, rel_type, dst_node):
    rows = edge_feats.shape[1]
    width = edge_feats.shape[2]
    relations = lax.axis_size("rel")
    groups = lax.axis_size("dom")
    slots = 2 * rows // relations
    half = relations // 2
    mine = lax.axis_index("rel")
    place = jnp.stack([mine, lax.axis_index("dom") * relations + mine]).astype(I32)
    def move(value, dom_bits, rel_bits):
        pairs = [
            (r * groups + g, (r ^ rel_bits) * groups + (g ^ dom_bits))
            for r in range(relations) for g in range(groups)
        ]
        return lax.ppermute(value, ("rel", "dom"), pairs)

    step = half // 4
    far = [list(range(half + k * step, half + (k + 1) * step)) for k in range(4)]
    first, kept = pack(
        place, rel_type.reshape(1, rows), dst_node, edge_feats[0], gain[None, :], relations, slots, half, 2 * step
    )
    held = {d: move(first[d - half], 0, d) for d in far[0] + far[1]}
    near = pack_more(kept, 0, half, slots)
    held[0] = near[0]
    held.update({d: move(near[d], 0, d) for d in range(1, half)})
    edges = [int(c * width) for c in CUTS]

    def run(turn, sums, last=False):
        blocks = [held[d] for d in turn]
        return expert(place, blocks, w_in[0], w_out[0], sums, groups, relations, edges if last else None)

    sums, token = run([0], None)
    for k in (2, 3):
        late = pack_more(kept, far[k][0], step, slots, [held[far[k - 2][-1]], token])
        held.update({d: move(block, 0, d) for d, block in zip(far[k], late)})
    for turn in (far[0] + far[1], list(range(1, half)), far[2]):
        sums, token = run(turn, sums)
    sums = run(far[3], sums, True)

    states = []
    for piece in sums:
        near = [piece[b].astype(F32) + move(piece[4 + b], 1, 0).astype(F32) for b in range(4)]
        total = near[0]
        for b in (3, 2, 1):
            total = total + move(near[b].astype(BF16), 2 * (b // 2), b % 2).astype(F32)
        total = total.reshape(half, NODE_DEV, -1)
        state = total[0]
        for z in range(half - 1, 0, -1):
            state = state + move(total[z].astype(BF16), 0, 2 * z).astype(F32)
        states.append(state)
    state = jnp.concatenate(states, axis=1)
    return (state * (1.0 / math.sqrt(rows / NODE_DEV)))[None]


def solution(mesh):
    in_specs = (
        P("dom", "rel", None),
        P(),
        P("rel", None, None),
        P("rel", None, None),
        P("dom", "rel", None),
        P("dom", "rel"),
    )
    out_specs = P("dom", "rel", None)
    return jax.shard_map(local, mesh=mesh, in_specs=in_specs, out_specs=out_specs, check_vma=False)
```

```python
import functools
import math

import jax
import jax.numpy as jnp
from jax import lax
from jax.experimental import pallas as pl
from jax.experimental.pallas import tpu as pltpu
from jax.sharding import PartitionSpec as P

NODE_DEV = 32
LANES = 128
EXTRA = 16
CUTS = (0.0, 1.0)
MIB = 1024 * 1024
VM = pl.BlockSpec(memory_space=pltpu.VMEM)
SM = pl.BlockSpec(memory_space=pltpu.SMEM)
HB = pl.BlockSpec(memory_space=pltpu.HBM)
F32 = jnp.float32
BF16 = jnp.bfloat16
I32 = jnp.int32


def write_blocks(first, slots, slot, coded, normed, blocks):
    rows, width = normed.shape
    for i, block in enumerate(blocks):
        at = lax.broadcasted_iota(I32, (slots, rows), 0) + (first + i) * slots
        pick = (slot == at).astype(BF16)
        picked = jnp.dot(pick, normed, preferred_element_type=F32).astype(BF16)
        for c in range(width // LANES):
            block[c * slots : (c + 1) * slots, :] = picked[:, c * LANES : (c + 1) * LANES]
        ids = lax.dot_general(coded, pick, (((1,), (1,)), ((), ())), preferred_element_type=F32)
        block[width // LANES * slots :, :slots] = ids.astype(BF16)


def pack_kernel(relations, slots, first, count, place_ref, kinds_hbm, dest_hbm, feats_hbm, gain_hbm, *refs):
    blocks, (normed_ref, slot_ref, coded_ref), scratch = (
        refs[:count], refs[count:-6], refs[-6:],
    )
    kinds_ref, dest_ref, gain_ref, feats_ref, sems, feat_sems = scratch
    rows, width = feats_ref.shape
    part = rows // 4
    small = [
        pltpu.make_async_copy(kinds_hbm, kinds_ref, sems.at[0]),
        pltpu.make_async_copy(dest_hbm, dest_ref, sems.at[1]),
        pltpu.make_async_copy(gain_hbm, gain_ref, sems.at[2]),
    ]
    large = [
        pltpu.make_async_copy(
            feats_hbm.at[pl.ds(i * part, part), :], feats_ref.at[pl.ds(i * part, part), :], feat_sems.at[i]
        )
        for i in range(4)
    ]
    for copy in small + large:
        copy.start()
    before = (
        lax.broadcasted_iota(I32, (rows, rows), 0) < lax.broadcasted_iota(I32, (rows, rows), 1)
    ).astype(BF16)
    for copy in small:
        copy.wait()
    offset = kinds_ref[...] ^ place_ref[0]
    marks = offset == lax.broadcasted_iota(I32, (max(relations, 16), rows), 0)
    count = jnp.dot(marks.astype(BF16), before, preferred_element_type=F32)
    rank = jnp.sum(jnp.where(marks, count, 0.0), axis=0, keepdims=True).astype(I32)
    slot = offset * slots + rank
    slot_ref[...] = slot
    dest = dest_ref[...]
    line = lax.broadcasted_iota(I32, (EXTRA, rows), 0)
    coded = jnp.where(
        line == 0, dest // NODE_DEV, jnp.where(line == 1, dest % NODE_DEV, jnp.where(line == 2, 1, 0))
    ).astype(BF16)
    coded_ref[...] = coded
    gain = gain_ref[...]
    for i in range(4):
        large[i].wait()
        at = slice(i * part, (i + 1) * part)
        feats = feats_ref[at, :].astype(F32)
        scale = lax.rsqrt(jnp.mean(feats * feats, axis=1, keepdims=True) + 1e-06)
        normed_ref[at, :] = (feats * scale * gain).astype(BF16)
    write_blocks(first, slots, slot, coded, normed_ref[...], blocks)


def pack_more_kernel(slots, first, count, normed_ref, slot_ref, coded_ref, *refs):
    write_blocks(first, slots, slot_ref[...], coded_ref[...], normed_ref[...], refs[-count:])


def pack_more(kept, first, count, slots, after=()):
    rows, width = kept[0].shape
    block = jax.ShapeDtypeStruct((width // LANES * slots + EXTRA, LANES), BF16)
    return pl.pallas_call(
        functools.partial(pack_more_kernel, slots, first, count),
        out_shape=[block] * count,
        in_specs=[VM] * 3 + [HB] * len(after),
        out_specs=[VM] * count,
        compiler_params=pltpu.CompilerParams(vmem_limit_bytes=16 * MIB),
        cost_estimate=pl.CostEstimate(flops=1, bytes_accessed=1, transcendentals=0),
        name="pack_more",
    )(*kept, *after)


def pack(place, kinds, dest, feats, gain, relations, slots, first, count):
    rows, width = feats.shape
    block = jax.ShapeDtypeStruct((width // LANES * slots + EXTRA, LANES), BF16)
    shapes = [block] * count + [
        jax.ShapeDtypeStruct((rows, width), BF16),
        jax.ShapeDtypeStruct((1, rows), I32),
        jax.ShapeDtypeStruct((EXTRA, rows), BF16),
    ]
    outs = pl.pallas_call(
        functools.partial(pack_kernel, relations, slots, first, count),
        out_shape=shapes,
        in_specs=[SM, HB, HB, HB, HB],
        out_specs=[VM] * len(shapes),
        scratch_shapes=[
            pltpu.VMEM((1, rows), I32),
            pltpu.VMEM((1, rows), I32),
            pltpu.VMEM((1, width), F32),
            pltpu.VMEM((rows, width), BF16),
            pltpu.SemaphoreType.DMA((3,)),
            pltpu.SemaphoreType.DMA((4,)),
        ],
        compiler_params=pltpu.CompilerParams(vmem_limit_bytes=16 * MIB),
        cost_estimate=pl.CostEstimate(flops=1, bytes_accessed=1, transcendentals=0),
        name="pack_far",
    )(place, *[pltpu.with_memory_space_constraint(a, pltpu.HBM) for a in (kinds, dest, feats, gain)])
    return outs[:count], outs[count:]


def gelu(x):
    return 0.5 * x * (1.0 + lax.erf(x * math.sqrt(0.5)))


def load_block(block_ref, x_ref, row, base, groups, relations):
    width = x_ref.shape[1]
    slots = (block_ref.shape[0] - EXTRA) * LANES // width
    for c in range(width // LANES):
        x_ref[row : row + slots, c * LANES : (c + 1) * LANES] = block_ref[c * slots : (c + 1) * slots, :]
    ids = block_ref[width // LANES * slots :, :slots].astype(F32).astype(I32)
    owner = ids[0:1] ^ base
    far = relations // 4
    y, z, f, g = owner % 2, owner // 2 % 2, owner // 4 % far, owner // relations
    at = (((((g % 2) * 2 + g // 2) * 2 + y) * 2 + z) * far + f) * NODE_DEV + ids[1:2]
    return jnp.where(ids[2:3] > 0, at, -1)


def up(x_ref, w_first_ref, hidden_ref):
    inner = w_first_ref.shape[1]
    part = 256

    def step(i, carry):
        at = pl.ds(pl.multiple_of(i * part, part), part)
        h = jnp.dot(x_ref[...], w_first_ref[:, at], preferred_element_type=F32)
        hidden_ref[:, at] = gelu(h).astype(BF16)
        return carry

    lax.fori_loop(0, inner // part, step, 0, unroll=8)


def down(hidden_ref, w_second_ref, table_ref, sums_ref, outs, left, right):
    part = 256
    nodes = table_ref.shape[0]
    piece = nodes // len(outs)
    messages = [
        jnp.dot(
            hidden_ref[...], w_second_ref[:, start : min(start + part, right)], preferred_element_type=F32
        ).astype(BF16)
        for start in range(left, right, part)
    ]
    for i, message in enumerate(messages):
        start = left + i * part
        size = message.shape[1]
        total = jnp.dot(table_ref[...], message, preferred_element_type=F32)
        if sums_ref is not None:
            total = total + sums_ref[:, start : start + size]
        for b, out in enumerate(outs):
            out[:, start - left : start - left + size] = total[b * piece : (b + 1) * piece].astype(out.dtype)


def expert_kernel(count, slots, groups, relations, has_sums, right, place_ref, *refs):
    blocks, refs = refs[:count], refs[count:]
    w_first_ref, w_second_ref, refs = refs[0], refs[1], refs[2:]
    sums_ref = None
    if has_sums:
        sums_ref, refs = refs[0], refs[1:]
    outs, (token_ref, hidden_ref, table_ref, x_ref) = refs[:-4], refs[-4:]
    token_ref[...] = jnp.zeros_like(token_ref)
    nodes = table_ref.shape[0]
    for i in range(count):
        line = load_block(blocks[i], x_ref, i * slots, place_ref[1], groups, relations)
        table_ref[:, i * slots : (i + 1) * slots] = (
            line == lax.broadcasted_iota(I32, (nodes, slots), 0)
        ).astype(BF16)
    up(x_ref, w_first_ref, hidden_ref)
    down(hidden_ref, w_second_ref, table_ref, sums_ref, outs, 0, right)


def more_kernel(left, right, hidden_ref, table_ref, w_second_ref, sums_ref, *outs):
    down(hidden_ref, w_second_ref, table_ref, sums_ref, outs, left, right)


def expert(place, blocks, w_first, w_second, sums, groups, relations, edges):
    count = len(blocks)
    width, inner = w_first.shape
    slots = (blocks[0].shape[0] - EXTRA) * LANES // width
    rows = count * slots
    nodes = groups * relations * NODE_DEV
    if edges is None:
        right, shapes = width, [jax.ShapeDtypeStruct((nodes, width), F32)]
    else:
        right, shapes = edges[1], [jax.ShapeDtypeStruct((nodes // 16, edges[1]), BF16)] * 16
    shapes.append(jax.ShapeDtypeStruct((8, LANES), F32))
    kept = [jax.ShapeDtypeStruct((rows, inner), BF16), jax.ShapeDtypeStruct((nodes, rows), BF16)]
    scratch = [pltpu.VMEM(s.shape, s.dtype) for s in kept]
    args = [place, *blocks, w_first, w_second] + ([] if sums is None else [sums])
    keep = edges is not None and len(edges) > 2
    params = pltpu.CompilerParams(vmem_limit_bytes=16 * MIB if relations <= 8 else 58 * MIB)
    outs = pl.pallas_call(
        functools.partial(expert_kernel, count, slots, groups, relations, sums is not None, right),
        out_shape=shapes + kept * keep,
        in_specs=[SM] + [VM] * (len(args) - 1),
        out_specs=[VM] * (len(shapes) + 2 * keep),
        scratch_shapes=scratch * (not keep) + [pltpu.VMEM((rows, width), BF16)],
        compiler_params=params,
        cost_estimate=pl.CostEstimate(flops=1, bytes_accessed=1, transcendentals=0),
        name="expert",
    )(*args)
    if edges is None:
        return outs
    pieces = [outs[:16]]
    for left, right in zip(edges[1:-1], edges[2:]):
        pieces.append(
            pl.pallas_call(
                functools.partial(more_kernel, left, right),
                out_shape=[jax.ShapeDtypeStruct((nodes // 16, right - left), BF16)] * 16,
                in_specs=[VM] * 4,
                out_specs=[VM] * 16,
                compiler_params=params,
                cost_estimate=pl.CostEstimate(flops=1, bytes_accessed=1, transcendentals=0),
                name="expert_more",
            )(outs[17], outs[18], w_second, sums)
        )
    return pieces


def local(edge_feats, gain, w_in, w_out, rel_type, dst_node):
    rows = edge_feats.shape[1]
    width = edge_feats.shape[2]
    relations = lax.axis_size("rel")
    groups = lax.axis_size("dom")
    slots = 2 * rows // relations
    half = relations // 2
    mine = lax.axis_index("rel")
    place = jnp.stack([mine, lax.axis_index("dom") * relations + mine]).astype(I32)
    def move(value, dom_bits, rel_bits):
        pairs = [
            (r * groups + g, (r ^ rel_bits) * groups + (g ^ dom_bits))
            for r in range(relations) for g in range(groups)
        ]
        return lax.ppermute(value, ("rel", "dom"), pairs)

    step = half // 4
    far = [list(range(half + k * step, half + (k + 1) * step)) for k in range(4)]
    first, kept = pack(
        place, rel_type.reshape(1, rows), dst_node, edge_feats[0], gain[None, :], relations, slots, half, 2 * step
    )
    held = {d: move(first[d - half], 0, d) for d in far[0] + far[1]}
    near = pack_more(kept, 0, half, slots)
    held[0] = near[0]
    held.update({d: move(near[d], 0, d) for d in range(1, half)})
    edges = [int(c * width) for c in CUTS]

    def run(turn, sums, last=False):
        blocks = [held[d] for d in turn]
        return expert(place, blocks, w_in[0], w_out[0], sums, groups, relations, edges if last else None)

    sums, token = run([0], None)
    for k in (2, 3):
        late = pack_more(kept, far[k][0], step, slots, [held[far[k - 2][-1]], token])
        held.update({d: move(block, 0, d) for d, block in zip(far[k], late)})
    for turn in (far[0] + [1], far[1] + list(range(2, half)), far[2]):
        sums, token = run(turn, sums)
    sums = run(far[3], sums, True)

    states = []
    for piece in sums:
        away = [move(jnp.concatenate(piece[b : b + 4]), 1, 0) for b in (8, 12)]
        lines = piece[0].shape[0]
        near = [
            piece[b].astype(F32) + away[b // 4][b % 4 * lines : (b % 4 + 1) * lines].astype(F32)
            for b in range(8)
        ]
        total = near[0]
        for b in (7, 6, 5, 3, 4, 2, 1):
            total = total + move(near[b].astype(BF16), 2 * (b // 4), b // 2 % 2 + 2 * (b % 2)).astype(F32)
        total = total.reshape(relations // 4, NODE_DEV, -1)
        state = total[0]
        for f in range(relations // 4 - 1, 0, -1):
            state = state + move(total[f].astype(BF16), 0, 4 * f).astype(F32)
        states.append(state)
    state = jnp.concatenate(states, axis=1)
    return (state * (1.0 / math.sqrt(rows / NODE_DEV)))[None]


def solution(mesh):
    in_specs = (
        P("dom", "rel", None),
        P(),
        P("rel", None, None),
        P("rel", None, None),
        P("dom", "rel", None),
        P("dom", "rel"),
    )
    out_specs = P("dom", "rel", None)
    return jax.shard_map(local, mesh=mesh, in_specs=in_specs, out_specs=out_specs, check_vma=False)
```

```python
import functools
import math

import jax
import jax.numpy as jnp
from jax import lax
from jax.experimental import pallas as pl
from jax.experimental.pallas import tpu as pltpu
from jax.sharding import PartitionSpec as P

NODE_DEV = 32
LANES = 128
EXTRA = 16
PAIRS = ((1, 2), (4, 3), (5, 6), (7, 0))
MIB = 1024 * 1024
VM = pl.BlockSpec(memory_space=pltpu.VMEM)
SM = pl.BlockSpec(memory_space=pltpu.SMEM)
HB = pl.BlockSpec(memory_space=pltpu.HBM)
F32 = jnp.float32
BF16 = jnp.bfloat16
I32 = jnp.int32


def write_blocks(labels, slots, slot, coded, normed, blocks):
    rows, width = normed.shape
    for label, block in zip(labels, blocks):
        at = lax.broadcasted_iota(I32, (slots, rows), 0) + label * slots
        pick = (slot == at).astype(BF16)
        picked = jnp.dot(pick, normed, preferred_element_type=F32).astype(BF16)
        for c in range(width // LANES):
            block[c * slots : (c + 1) * slots, :] = picked[:, c * LANES : (c + 1) * LANES]
        ids = lax.dot_general(coded, pick, (((1,), (1,)), ((), ())), preferred_element_type=F32)
        block[width // LANES * slots :, :slots] = ids.astype(BF16)


def pack_kernel(relations, slots, labels, place_ref, kinds_hbm, dest_hbm, feats_hbm, gain_hbm, *refs):
    blocks, (normed_ref, slot_ref, coded_ref), scratch = (
        refs[: len(labels)], refs[len(labels) : -6], refs[-6:],
    )
    kinds_ref, dest_ref, gain_ref, feats_ref, sems, feat_sems = scratch
    rows, width = feats_ref.shape
    part = rows // 4
    small = [
        pltpu.make_async_copy(kinds_hbm, kinds_ref, sems.at[0]),
        pltpu.make_async_copy(dest_hbm, dest_ref, sems.at[1]),
        pltpu.make_async_copy(gain_hbm, gain_ref, sems.at[2]),
    ]
    large = [
        pltpu.make_async_copy(
            feats_hbm.at[pl.ds(i * part, part), :], feats_ref.at[pl.ds(i * part, part), :], feat_sems.at[i]
        )
        for i in range(4)
    ]
    for copy in small + large:
        copy.start()
    before = (
        lax.broadcasted_iota(I32, (rows, rows), 0) < lax.broadcasted_iota(I32, (rows, rows), 1)
    ).astype(BF16)
    for copy in small:
        copy.wait()
    offset = kinds_ref[...] ^ place_ref[0]
    marks = offset == lax.broadcasted_iota(I32, (max(relations, 16), rows), 0)
    count = jnp.dot(marks.astype(BF16), before, preferred_element_type=F32)
    rank = jnp.sum(jnp.where(marks, count, 0.0), axis=0, keepdims=True).astype(I32)
    slot = offset * slots + rank
    slot_ref[...] = slot
    dest = dest_ref[...]
    line = lax.broadcasted_iota(I32, (EXTRA, rows), 0)
    coded = jnp.where(
        line == 0, dest // NODE_DEV, jnp.where(line == 1, dest % NODE_DEV, jnp.where(line == 2, 1, 0))
    ).astype(BF16)
    coded_ref[...] = coded
    gain = gain_ref[...]
    for i in range(4):
        large[i].wait()
        at = slice(i * part, (i + 1) * part)
        feats = feats_ref[at, :].astype(F32)
        scale = lax.rsqrt(jnp.mean(feats * feats, axis=1, keepdims=True) + 1e-06)
        normed_ref[at, :] = (feats * scale * gain).astype(BF16)
    write_blocks(labels, slots, slot, coded, normed_ref[...], blocks)


def pack_more_kernel(slots, labels, normed_ref, slot_ref, coded_ref, *refs):
    write_blocks(labels, slots, slot_ref[...], coded_ref[...], normed_ref[...], refs[-len(labels) :])


def pack_more(kept, labels, slots, after=()):
    rows, width = kept[0].shape
    block = jax.ShapeDtypeStruct((width // LANES * slots + EXTRA, LANES), BF16)
    return pl.pallas_call(
        functools.partial(pack_more_kernel, slots, labels),
        out_shape=[block] * len(labels),
        in_specs=[VM] * 3 + [HB] * len(after),
        out_specs=[VM] * len(labels),
        compiler_params=pltpu.CompilerParams(vmem_limit_bytes=16 * MIB),
        cost_estimate=pl.CostEstimate(flops=1, bytes_accessed=1, transcendentals=0),
        name="pack_more",
    )(*kept, *after)


def pack(place, kinds, dest, feats, gain, relations, slots, labels):
    rows, width = feats.shape
    block = jax.ShapeDtypeStruct((width // LANES * slots + EXTRA, LANES), BF16)
    shapes = [block] * len(labels) + [
        jax.ShapeDtypeStruct((rows, width), BF16),
        jax.ShapeDtypeStruct((1, rows), I32),
        jax.ShapeDtypeStruct((EXTRA, rows), BF16),
    ]
    outs = pl.pallas_call(
        functools.partial(pack_kernel, relations, slots, labels),
        out_shape=shapes,
        in_specs=[SM, HB, HB, HB, HB],
        out_specs=[VM] * len(shapes),
        scratch_shapes=[
            pltpu.VMEM((1, rows), I32),
            pltpu.VMEM((1, rows), I32),
            pltpu.VMEM((1, width), F32),
            pltpu.VMEM((rows, width), BF16),
            pltpu.SemaphoreType.DMA((3,)),
            pltpu.SemaphoreType.DMA((4,)),
        ],
        compiler_params=pltpu.CompilerParams(vmem_limit_bytes=16 * MIB),
        cost_estimate=pl.CostEstimate(flops=1, bytes_accessed=1, transcendentals=0),
        name="pack_far",
    )(place, *[pltpu.with_memory_space_constraint(a, pltpu.HBM) for a in (kinds, dest, feats, gain)])
    return outs[: len(labels)], outs[len(labels) :]


def gelu(x):
    return 0.5 * x * (1.0 + lax.erf(x * math.sqrt(0.5)))


def load_block(block_ref, x_ref, row, base, groups, relations):
    width = x_ref.shape[1]
    slots = (block_ref.shape[0] - EXTRA) * LANES // width
    for c in range(width // LANES):
        x_ref[row : row + slots, c * LANES : (c + 1) * LANES] = block_ref[c * slots : (c + 1) * slots, :]
    ids = block_ref[width // LANES * slots :, :slots].astype(F32).astype(I32)
    owner = ids[0:1] ^ base
    far = relations // 4
    y, z, f, g = owner % 2, owner // 2 % 2, owner // 4 % far, owner // relations
    at = (((((g % 2) * 2 + g // 2) * 2 + y) * 2 + z) * far + f) * NODE_DEV + ids[1:2]
    return jnp.where(ids[2:3] > 0, at, -1)


def up(x_ref, w_first_ref, hidden_ref):
    inner = w_first_ref.shape[1]
    part = 256

    def step(i, carry):
        at = pl.ds(pl.multiple_of(i * part, part), part)
        h = jnp.dot(x_ref[...], w_first_ref[:, at], preferred_element_type=F32)
        hidden_ref[:, at] = gelu(h).astype(BF16)
        return carry

    lax.fori_loop(0, inner // part, step, 0, unroll=8)


def down(hidden_ref, w_second_ref, table_ref, sums_ref, outs):
    part = 256
    width = w_second_ref.shape[1]
    piece = table_ref.shape[0] // len(outs)
    messages = [
        jnp.dot(hidden_ref[...], w_second_ref[:, at : at + part], preferred_element_type=F32).astype(BF16)
        for at in range(0, width, part)
    ]
    for i, message in enumerate(messages):
        columns = slice(i * part, (i + 1) * part)
        total = jnp.dot(table_ref[...], message, preferred_element_type=F32)
        if sums_ref is not None:
            total = total + sums_ref[:, columns]
        for b, out in enumerate(outs):
            out[:, columns] = total[b * piece : (b + 1) * piece].astype(out.dtype)


def expert_kernel(count, slots, groups, relations, has_sums, last, place_ref, *refs):
    blocks, refs = refs[:count], refs[count:]
    w_first_ref, w_second_ref, refs = refs[0], refs[1], refs[2:]
    sums_ref = None
    if has_sums:
        sums_ref, refs = refs[0], refs[1:]
    outs, (hidden_ref, table_ref, x_ref) = refs[:-3], refs[-3:]
    if not last:
        outs[-1][...] = jnp.zeros_like(outs[-1])
        outs = outs[:-1]
    nodes = table_ref.shape[0]
    for i in range(count):
        line = load_block(blocks[i], x_ref, i * slots, place_ref[1], groups, relations)
        table_ref[:, i * slots : (i + 1) * slots] = (
            line == lax.broadcasted_iota(I32, (nodes, slots), 0)
        ).astype(BF16)
    up(x_ref, w_first_ref, hidden_ref)
    down(hidden_ref, w_second_ref, table_ref, sums_ref, outs)


def expert(place, blocks, w_first, w_second, sums, groups, relations, last):
    count = len(blocks)
    width, inner = w_first.shape
    slots = (blocks[0].shape[0] - EXTRA) * LANES // width
    rows = count * slots
    nodes = groups * relations * NODE_DEV
    if last:
        shapes = [jax.ShapeDtypeStruct((nodes // 16, width), BF16)] * 16
    else:
        shapes = [jax.ShapeDtypeStruct((nodes, width), F32), jax.ShapeDtypeStruct((8, LANES), F32)]
    args = [place, *blocks, w_first, w_second] + ([] if sums is None else [sums])
    return pl.pallas_call(
        functools.partial(expert_kernel, count, slots, groups, relations, sums is not None, last),
        out_shape=shapes,
        in_specs=[SM] + [VM] * (len(args) - 1),
        out_specs=[VM] * len(shapes),
        scratch_shapes=[
            pltpu.VMEM((rows, inner), BF16), pltpu.VMEM((nodes, rows), BF16), pltpu.VMEM((rows, width), BF16),
        ],
        compiler_params=pltpu.CompilerParams(vmem_limit_bytes=(16 if relations <= 8 else 58) * MIB),
        cost_estimate=pl.CostEstimate(flops=1, bytes_accessed=1, transcendentals=0),
        name="expert",
    )(*args)


def local(edge_feats, gain, w_in, w_out, rel_type, dst_node):
    rows = edge_feats.shape[1]
    width = edge_feats.shape[2]
    relations = lax.axis_size("rel")
    groups = lax.axis_size("dom")
    slots = 2 * rows // relations
    half = relations // 2
    mine = lax.axis_index("rel")
    place = jnp.stack([mine, lax.axis_index("dom") * relations + mine]).astype(I32)

    def move(value, dom_bits, rel_bits):
        pairs = [
            (r * groups + g, (r ^ rel_bits) * groups + (g ^ dom_bits))
            for r in range(relations) for g in range(groups)
        ]
        return lax.ppermute(value, ("rel", "dom"), pairs)

    step = half // 4
    far = [list(range(half + k * step, half + (k + 1) * step)) for k in range(4)]
    first, kept = pack(
        place, rel_type.reshape(1, rows), dst_node, edge_feats[0], gain[None, :], relations, slots, far[0] + far[1]
    )
    held = {d: move(block, 0, d) for d, block in zip(far[0] + far[1], first)}
    near = pack_more(kept, list(range(half)), slots)
    held[0] = near[0]
    held.update({d: move(near[d], 0, d) for d in range(1, half)})

    def run(turn, sums, last=False):
        blocks = [held[d] for d in turn]
        return expert(place, blocks, w_in[0], w_out[0], sums, groups, relations, last)

    sums, token = run([0], None)
    for k in (2, 3):
        late = pack_more(kept, far[k], slots, [held[far[k - 2][-1]], token])
        held.update({d: move(block, 0, d) for d, block in zip(far[k], late)})
    for turn in (far[0] + [1], far[1] + list(range(2, half)), far[2]):
        sums, token = run(turn, sums)
    sums = run(far[3], sums, True)

    lines = sums[0].shape[0]
    away = {}
    for pair in PAIRS:
        got = move(jnp.concatenate([sums[8 + b] for b in pair]), 1, 0)
        away.update({b: got[i * lines : (i + 1) * lines] for i, b in enumerate(pair)})
    near = [sums[b].astype(F32) + away[b].astype(F32) for b in range(8)]
    total = near[0]
    for b in (7, 6, 5, 3, 4, 2, 1):
        total = total + move(near[b].astype(BF16), 2 * (b // 4), b // 2 % 2 + 2 * (b % 2)).astype(F32)
    total = total.reshape(relations // 4, NODE_DEV, -1)
    state = total[0]
    for f in range(relations // 4 - 1, 0, -1):
        state = state + move(total[f].astype(BF16), 0, 4 * f).astype(F32)
    return (state * (1.0 / math.sqrt(rows / NODE_DEV)))[None]


def solution(mesh):
    in_specs = (
        P("dom", "rel", None),
        P(),
        P("rel", None, None),
        P("rel", None, None),
        P("dom", "rel", None),
        P("dom", "rel"),
    )
    out_specs = P("dom", "rel", None)
    return jax.shard_map(local, mesh=mesh, in_specs=in_specs, out_specs=out_specs, check_vma=False)
```

```python
import functools
import math

import jax
import jax.numpy as jnp
from jax import lax
from jax.experimental import pallas as pl
from jax.experimental.pallas import tpu as pltpu
from jax.sharding import PartitionSpec as P

NODE_DEV = 32
LANES = 128
EXTRA = 16
PAIRS = ((1, 2), (4, 3), (5, 6), (7, 0))
MIB = 1024 * 1024
VM = pl.BlockSpec(memory_space=pltpu.VMEM)
SM = pl.BlockSpec(memory_space=pltpu.SMEM)
HB = pl.BlockSpec(memory_space=pltpu.HBM)
F32 = jnp.float32
BF16 = jnp.bfloat16
I32 = jnp.int32


def write_blocks(labels, slots, slot, coded, normed, blocks):
    rows, width = normed.shape
    for label, block in zip(labels, blocks):
        at = lax.broadcasted_iota(I32, (slots, rows), 0) + label * slots
        pick = (slot == at).astype(BF16)
        picked = jnp.dot(pick, normed, preferred_element_type=F32).astype(BF16)
        for c in range(width // LANES):
            block[c * slots : (c + 1) * slots, :] = picked[:, c * LANES : (c + 1) * LANES]
        ids = lax.dot_general(coded, pick, (((1,), (1,)), ((), ())), preferred_element_type=F32)
        block[width // LANES * slots :, :slots] = ids.astype(BF16)


def pack_kernel(relations, slots, labels, place_ref, kinds_hbm, dest_hbm, feats_hbm, gain_hbm, *refs):
    blocks, (normed_ref, slot_ref, coded_ref), scratch = (
        refs[: len(labels)], refs[len(labels) : -6], refs[-6:],
    )
    kinds_ref, dest_ref, gain_ref, feats_ref, sems, feat_sems = scratch
    rows, width = feats_ref.shape
    parts = 2
    part = rows // parts
    small = [
        pltpu.make_async_copy(kinds_hbm, kinds_ref, sems.at[0]),
        pltpu.make_async_copy(dest_hbm, dest_ref, sems.at[1]),
        pltpu.make_async_copy(gain_hbm, gain_ref, sems.at[2]),
    ]
    large = [
        pltpu.make_async_copy(
            feats_hbm.at[pl.ds(i * part, part), :], feats_ref.at[pl.ds(i * part, part), :], feat_sems.at[i]
        )
        for i in range(parts)
    ]
    for copy in small + large:
        copy.start()
    before = (
        lax.broadcasted_iota(I32, (rows, rows), 0) < lax.broadcasted_iota(I32, (rows, rows), 1)
    ).astype(BF16)
    for copy in small:
        copy.wait()
    offset = kinds_ref[...] ^ place_ref[0]
    marks = offset == lax.broadcasted_iota(I32, (max(relations, 16), rows), 0)
    count = jnp.dot(marks.astype(BF16), before, preferred_element_type=F32)
    rank = jnp.sum(jnp.where(marks, count, 0.0), axis=0, keepdims=True).astype(I32)
    slot = offset * slots + rank
    slot_ref[...] = slot
    dest = dest_ref[...]
    line = lax.broadcasted_iota(I32, (EXTRA, rows), 0)
    coded = jnp.where(
        line == 0, dest // NODE_DEV, jnp.where(line == 1, dest % NODE_DEV, jnp.where(line == 2, 1, 0))
    ).astype(BF16)
    coded_ref[...] = coded
    gain = gain_ref[...]
    for i in range(parts):
        large[i].wait()
        at = slice(i * part, (i + 1) * part)
        feats = feats_ref[at, :].astype(F32)
        scale = lax.rsqrt(jnp.mean(feats * feats, axis=1, keepdims=True) + 1e-06)
        normed_ref[at, :] = (feats * scale * gain).astype(BF16)
    write_blocks(labels, slots, slot, coded, normed_ref[...], blocks)


def pack_more_kernel(slots, labels, normed_ref, slot_ref, coded_ref, *refs):
    write_blocks(labels, slots, slot_ref[...], coded_ref[...], normed_ref[...], refs[-len(labels) :])


def pack_more(kept, labels, slots, after=()):
    rows, width = kept[0].shape
    block = jax.ShapeDtypeStruct((width // LANES * slots + EXTRA, LANES), BF16)
    return pl.pallas_call(
        functools.partial(pack_more_kernel, slots, labels),
        out_shape=[block] * len(labels),
        in_specs=[VM] * 3 + [HB] * len(after),
        out_specs=[VM] * len(labels),
        compiler_params=pltpu.CompilerParams(vmem_limit_bytes=16 * MIB),
        cost_estimate=pl.CostEstimate(flops=1, bytes_accessed=1, transcendentals=0),
        name="pack_more",
    )(*kept, *after)


def pack(place, kinds, dest, feats, gain, relations, slots, labels):
    rows, width = feats.shape
    block = jax.ShapeDtypeStruct((width // LANES * slots + EXTRA, LANES), BF16)
    shapes = [block] * len(labels) + [
        jax.ShapeDtypeStruct((rows, width), BF16),
        jax.ShapeDtypeStruct((1, rows), I32),
        jax.ShapeDtypeStruct((EXTRA, rows), BF16),
    ]
    outs = pl.pallas_call(
        functools.partial(pack_kernel, relations, slots, labels),
        out_shape=shapes,
        in_specs=[SM, HB, HB, HB, HB],
        out_specs=[VM] * len(shapes),
        scratch_shapes=[
            pltpu.VMEM((1, rows), I32),
            pltpu.VMEM((1, rows), I32),
            pltpu.VMEM((1, width), F32),
            pltpu.VMEM((rows, width), BF16),
            pltpu.SemaphoreType.DMA((3,)),
            pltpu.SemaphoreType.DMA((2,)),
        ],
        compiler_params=pltpu.CompilerParams(vmem_limit_bytes=16 * MIB),
        cost_estimate=pl.CostEstimate(flops=1, bytes_accessed=1, transcendentals=0),
        name="pack_far",
    )(place, *[pltpu.with_memory_space_constraint(a, pltpu.HBM) for a in (kinds, dest, feats, gain)])
    return outs[: len(labels)], outs[len(labels) :]


def gelu(x):
    return 0.5 * x * (1.0 + lax.erf(x * math.sqrt(0.5)))


def load_block(block_ref, x_ref, row, base, groups, relations):
    width = x_ref.shape[1]
    slots = (block_ref.shape[0] - EXTRA) * LANES // width
    for c in range(width // LANES):
        x_ref[row : row + slots, c * LANES : (c + 1) * LANES] = block_ref[c * slots : (c + 1) * slots, :]
    ids = block_ref[width // LANES * slots :, :slots].astype(F32).astype(I32)
    owner = ids[0:1] ^ base
    far = relations // 4
    y, z, f, g = owner % 2, owner // 2 % 2, owner // 4 % far, owner // relations
    at = (((((g % 2) * 2 + g // 2) * 2 + y) * 2 + z) * far + f) * NODE_DEV + ids[1:2]
    return jnp.where(ids[2:3] > 0, at, -1)


def up(x_ref, w_first_ref, hidden_ref):
    inner = w_first_ref.shape[1]
    part = 256

    def step(i, carry):
        at = pl.ds(pl.multiple_of(i * part, part), part)
        h = jnp.dot(x_ref[...], w_first_ref[:, at], preferred_element_type=F32)
        hidden_ref[:, at] = gelu(h).astype(BF16)
        return carry

    lax.fori_loop(0, inner // part, step, 0, unroll=8)


def down(hidden_ref, w_second_ref, table_ref, sums_ref, outs):
    part = 256
    width = w_second_ref.shape[1]
    piece = table_ref.shape[0] // len(outs)
    messages = [
        jnp.dot(hidden_ref[...], w_second_ref[:, at : at + part], preferred_element_type=F32).astype(BF16)
        for at in range(0, width, part)
    ]
    for i, message in enumerate(messages):
        columns = slice(i * part, (i + 1) * part)
        total = jnp.dot(table_ref[...], message, preferred_element_type=F32)
        if sums_ref is not None:
            total = total + sums_ref[:, columns]
        for b, out in enumerate(outs):
            out[:, columns] = total[b * piece : (b + 1) * piece].astype(out.dtype)


def expert_kernel(count, slots, groups, relations, has_sums, last, place_ref, *refs):
    blocks, refs = refs[:count], refs[count:]
    w_first_ref, w_second_ref, refs = refs[0], refs[1], refs[2:]
    sums_ref = None
    if has_sums:
        sums_ref, refs = refs[0], refs[1:]
    outs, (hidden_ref, table_ref, x_ref) = refs[:-3], refs[-3:]
    if not last:
        outs[-1][...] = jnp.zeros_like(outs[-1])
        outs = outs[:-1]
    nodes = table_ref.shape[0]
    for i in range(count):
        line = load_block(blocks[i], x_ref, i * slots, place_ref[1], groups, relations)
        table_ref[:, i * slots : (i + 1) * slots] = (
            line == lax.broadcasted_iota(I32, (nodes, slots), 0)
        ).astype(BF16)
    up(x_ref, w_first_ref, hidden_ref)
    down(hidden_ref, w_second_ref, table_ref, sums_ref, outs)


def expert(place, blocks, w_first, w_second, sums, groups, relations, last):
    count = len(blocks)
    width, inner = w_first.shape
    slots = (blocks[0].shape[0] - EXTRA) * LANES // width
    rows = count * slots
    nodes = groups * relations * NODE_DEV
    if last:
        shapes = [jax.ShapeDtypeStruct((nodes // 16, width), BF16)] * 16
    else:
        shapes = [jax.ShapeDtypeStruct((nodes, width), F32), jax.ShapeDtypeStruct((8, LANES), F32)]
    args = [place, *blocks, w_first, w_second] + ([] if sums is None else [sums])
    return pl.pallas_call(
        functools.partial(expert_kernel, count, slots, groups, relations, sums is not None, last),
        out_shape=shapes,
        in_specs=[SM] + [VM] * (len(args) - 1),
        out_specs=[VM] * len(shapes),
        scratch_shapes=[
            pltpu.VMEM((rows, inner), BF16), pltpu.VMEM((nodes, rows), BF16), pltpu.VMEM((rows, width), BF16),
        ],
        compiler_params=pltpu.CompilerParams(vmem_limit_bytes=(16 if relations <= 8 else 58) * MIB),
        cost_estimate=pl.CostEstimate(flops=1, bytes_accessed=1, transcendentals=0),
        name="expert",
    )(*args)


def local(edge_feats, gain, w_in, w_out, rel_type, dst_node):
    rows = edge_feats.shape[1]
    width = edge_feats.shape[2]
    relations = lax.axis_size("rel")
    groups = lax.axis_size("dom")
    slots = 2 * rows // relations
    half = relations // 2
    mine = lax.axis_index("rel")
    place = jnp.stack([mine, lax.axis_index("dom") * relations + mine]).astype(I32)

    def move(value, dom_bits, rel_bits):
        pairs = [
            (r * groups + g, (r ^ rel_bits) * groups + (g ^ dom_bits))
            for r in range(relations) for g in range(groups)
        ]
        return lax.ppermute(value, ("rel", "dom"), pairs)

    step = half // 4
    far = [list(range(half + k * step, half + (k + 1) * step)) for k in range(4)]
    early, rest = far[0], list(range(half)) + far[1]
    first, kept = pack(
        place, rel_type.reshape(1, rows), dst_node, edge_feats[0], gain[None, :], relations, slots, early
    )
    held = {d: move(block, 0, d) for d, block in zip(early, first)}
    held.update({d: move(block, 0, d) if d else block for d, block in zip(rest, pack_more(kept, rest, slots))})

    def run(turn, sums, last=False):
        blocks = [held[d] for d in turn]
        return expert(place, blocks, w_in[0], w_out[0], sums, groups, relations, last)

    sums, token = run([0], None)
    for k in (2, 3):
        late = pack_more(kept, far[k], slots, [held[far[k - 2][-1]], token])
        held.update({d: move(block, 0, d) for d, block in zip(far[k], late)})
    for turn in (far[0] + [1], far[1] + list(range(2, half)), far[2]):
        sums, token = run(turn, sums)
    sums = run(far[3], sums, True)

    lines = sums[0].shape[0]
    away = {}
    for pair in PAIRS:
        got = move(jnp.concatenate([sums[8 + b] for b in pair]), 1, 0)
        away.update({b: got[i * lines : (i + 1) * lines] for i, b in enumerate(pair)})
    near = [sums[b].astype(F32) + away[b].astype(F32) for b in range(8)]
    total = near[0]
    for b in (7, 6, 5, 3, 4, 2, 1):
        total = total + move(near[b].astype(BF16), 2 * (b // 4), b // 2 % 2 + 2 * (b % 2)).astype(F32)
    total = total.reshape(relations // 4, NODE_DEV, -1)
    state = total[0]
    for f in range(relations // 4 - 1, 0, -1):
        state = state + move(total[f].astype(BF16), 0, 4 * f).astype(F32)
    return (state * (1.0 / math.sqrt(rows / NODE_DEV)))[None]


def solution(mesh):
    in_specs = (
        P("dom", "rel", None),
        P(),
        P("rel", None, None),
        P("rel", None, None),
        P("dom", "rel", None),
        P("dom", "rel"),
    )
    out_specs = P("dom", "rel", None)
    return jax.shard_map(local, mesh=mesh, in_specs=in_specs, out_specs=out_specs, check_vma=False)
```

```python
import functools
import math

import jax
import jax.numpy as jnp
from jax import lax
from jax.experimental import pallas as pl
from jax.experimental.pallas import tpu as pltpu
from jax.sharding import PartitionSpec as P

NODE_DEV = 32
LANES = 128
EXTRA = 16
PAIRS = ((1, 2), (4, 3), (5, 6), (7, 0))
MIB = 1024 * 1024
VM = pl.BlockSpec(memory_space=pltpu.VMEM)
SM = pl.BlockSpec(memory_space=pltpu.SMEM)
HB = pl.BlockSpec(memory_space=pltpu.HBM)
F32 = jnp.float32
BF16 = jnp.bfloat16
I32 = jnp.int32


def write_blocks(labels, slots, slot, coded, normed, blocks):
    rows, width = normed.shape
    for label, block in zip(labels, blocks):
        at = lax.broadcasted_iota(I32, (slots, rows), 0) + label * slots
        pick = (slot == at).astype(BF16)
        picked = jnp.dot(pick, normed, preferred_element_type=F32).astype(BF16)
        for c in range(width // LANES):
            block[c * slots : (c + 1) * slots, :] = picked[:, c * LANES : (c + 1) * LANES]
        ids = lax.dot_general(coded, pick, (((1,), (1,)), ((), ())), preferred_element_type=F32)
        block[width // LANES * slots :, :slots] = ids.astype(BF16)


def pack_kernel(relations, slots, labels, place_ref, kinds_hbm, dest_hbm, feats_hbm, gain_hbm, *refs):
    blocks, (normed_ref, slot_ref, coded_ref), scratch = (
        refs[: len(labels)], refs[len(labels) : -6], refs[-6:],
    )
    kinds_ref, dest_ref, gain_ref, feats_ref, sems, feat_sems = scratch
    rows, width = feats_ref.shape
    parts = 2
    part = rows // parts
    small = [
        pltpu.make_async_copy(kinds_hbm, kinds_ref, sems.at[0]),
        pltpu.make_async_copy(dest_hbm, dest_ref, sems.at[1]),
        pltpu.make_async_copy(gain_hbm, gain_ref, sems.at[2]),
    ]
    large = [
        pltpu.make_async_copy(
            feats_hbm.at[pl.ds(i * part, part), :], feats_ref.at[pl.ds(i * part, part), :], feat_sems.at[i]
        )
        for i in range(parts)
    ]
    for copy in small + large:
        copy.start()
    before = (
        lax.broadcasted_iota(I32, (rows, rows), 0) < lax.broadcasted_iota(I32, (rows, rows), 1)
    ).astype(BF16)
    for copy in small:
        copy.wait()
    offset = kinds_ref[...] ^ place_ref[0]
    marks = offset == lax.broadcasted_iota(I32, (max(relations, 16), rows), 0)
    count = jnp.dot(marks.astype(BF16), before, preferred_element_type=F32)
    rank = jnp.sum(jnp.where(marks, count, 0.0), axis=0, keepdims=True).astype(I32)
    slot = offset * slots + rank
    slot_ref[...] = slot
    dest = dest_ref[...]
    line = lax.broadcasted_iota(I32, (EXTRA, rows), 0)
    coded = jnp.where(
        line == 0, dest // NODE_DEV, jnp.where(line == 1, dest % NODE_DEV, jnp.where(line == 2, 1, 0))
    ).astype(BF16)
    coded_ref[...] = coded
    gain = gain_ref[...]
    for i in range(parts):
        large[i].wait()
        at = slice(i * part, (i + 1) * part)
        feats = feats_ref[at, :].astype(F32)
        scale = lax.rsqrt(jnp.mean(feats * feats, axis=1, keepdims=True) + 1e-06)
        normed_ref[at, :] = (feats * scale * gain).astype(BF16)
    write_blocks(labels, slots, slot, coded, normed_ref[...], blocks)


def pack_more_kernel(slots, labels, normed_ref, slot_ref, coded_ref, *refs):
    write_blocks(labels, slots, slot_ref[...], coded_ref[...], normed_ref[...], refs[-len(labels) :])


def pack_more(kept, labels, slots, after=()):
    rows, width = kept[0].shape
    block = jax.ShapeDtypeStruct((width // LANES * slots + EXTRA, LANES), BF16)
    return pl.pallas_call(
        functools.partial(pack_more_kernel, slots, labels),
        out_shape=[block] * len(labels),
        in_specs=[VM] * 3 + [HB] * len(after),
        out_specs=[VM] * len(labels),
        compiler_params=pltpu.CompilerParams(vmem_limit_bytes=16 * MIB),
        cost_estimate=pl.CostEstimate(flops=1, bytes_accessed=1, transcendentals=0),
        name="pack_more",
    )(*kept, *after)


def pack(place, kinds, dest, feats, gain, relations, slots, labels):
    rows, width = feats.shape
    block = jax.ShapeDtypeStruct((width // LANES * slots + EXTRA, LANES), BF16)
    shapes = [block] * len(labels) + [
        jax.ShapeDtypeStruct((rows, width), BF16),
        jax.ShapeDtypeStruct((1, rows), I32),
        jax.ShapeDtypeStruct((EXTRA, rows), BF16),
    ]
    outs = pl.pallas_call(
        functools.partial(pack_kernel, relations, slots, labels),
        out_shape=shapes,
        in_specs=[SM, HB, HB, HB, HB],
        out_specs=[VM] * len(shapes),
        scratch_shapes=[
            pltpu.VMEM((1, rows), I32),
            pltpu.VMEM((1, rows), I32),
            pltpu.VMEM((1, width), F32),
            pltpu.VMEM((rows, width), BF16),
            pltpu.SemaphoreType.DMA((3,)),
            pltpu.SemaphoreType.DMA((2,)),
        ],
        compiler_params=pltpu.CompilerParams(vmem_limit_bytes=16 * MIB),
        cost_estimate=pl.CostEstimate(flops=1, bytes_accessed=1, transcendentals=0),
        name="pack_far",
    )(place, *[pltpu.with_memory_space_constraint(a, pltpu.HBM) for a in (kinds, dest, feats, gain)])
    return outs[: len(labels)], outs[len(labels) :]


def gelu(x):
    return 0.5 * x * (1.0 + lax.erf(x * math.sqrt(0.5)))


def load_block(block_ref, x_ref, row, base, groups, relations):
    width = x_ref.shape[1]
    slots = (block_ref.shape[0] - EXTRA) * LANES // width
    for c in range(width // LANES):
        x_ref[row : row + slots, c * LANES : (c + 1) * LANES] = block_ref[c * slots : (c + 1) * slots, :]
    ids = block_ref[width // LANES * slots :, :slots].astype(F32).astype(I32)
    owner = ids[0:1] ^ base
    far = relations // 4
    y, z, f, g = owner % 2, owner // 2 % 2, owner // 4 % far, owner // relations
    at = (((((g % 2) * 2 + g // 2) * 2 + y) * 2 + z) * far + f) * NODE_DEV + ids[1:2]
    return jnp.where(ids[2:3] > 0, at, -1)


def up(x_ref, w_first_ref, hidden_ref):
    inner = w_first_ref.shape[1]
    part = 256

    def step(i, carry):
        at = pl.ds(pl.multiple_of(i * part, part), part)
        h = jnp.dot(x_ref[...], w_first_ref[:, at], preferred_element_type=F32)
        hidden_ref[:, at] = gelu(h).astype(BF16)
        return carry

    lax.fori_loop(0, inner // part, step, 0, unroll=8)


def down(hidden_ref, w_second_ref, table_ref, sums_ref, outs, kept):
    part = 256
    width = w_second_ref.shape[1]
    nodes = table_ref.shape[0]
    start = nodes // 2 if kept else 0
    messages = [
        jnp.dot(hidden_ref[...], w_second_ref[:, at : at + part], preferred_element_type=F32).astype(BF16)
        for at in range(0, width, part)
    ]
    for i, message in enumerate(messages):
        columns = slice(i * part, (i + 1) * part)
        if kept:
            kept[0][:, columns] = message
        add(table_ref[start:, :], message, sums_ref, start, columns, outs)
    if kept:
        kept[1][...] = table_ref[:start, :]


def add(table, message, sums_ref, start, columns, outs):
    total = jnp.dot(table, message, preferred_element_type=F32)
    piece = table.shape[0] // len(outs)
    if sums_ref is not None:
        total = total + sums_ref[start : start + table.shape[0], columns]
    for b, out in enumerate(outs):
        out[:, columns] = total[b * piece : (b + 1) * piece].astype(out.dtype)


def rest_kernel(messages_ref, table_ref, sums_ref, *outs):
    part = 256
    for at in range(0, messages_ref.shape[1], part):
        columns = slice(at, at + part)
        add(table_ref[...], messages_ref[:, columns], sums_ref, 0, columns, outs)


def expert_kernel(count, slots, groups, relations, has_sums, last, place_ref, *refs):
    blocks, refs = refs[:count], refs[count:]
    w_first_ref, w_second_ref, refs = refs[0], refs[1], refs[2:]
    sums_ref = None
    if has_sums:
        sums_ref, refs = refs[0], refs[1:]
    outs, (hidden_ref, table_ref, x_ref) = refs[:-3], refs[-3:]
    kept = ()
    if last:
        outs, kept = outs[:8], outs[8:]
    else:
        outs[-1][...] = jnp.zeros_like(outs[-1])
        outs = outs[:-1]
    nodes = table_ref.shape[0]
    for i in range(count):
        line = load_block(blocks[i], x_ref, i * slots, place_ref[1], groups, relations)
        table_ref[:, i * slots : (i + 1) * slots] = (
            line == lax.broadcasted_iota(I32, (nodes, slots), 0)
        ).astype(BF16)
    up(x_ref, w_first_ref, hidden_ref)
    down(hidden_ref, w_second_ref, table_ref, sums_ref, outs, kept)


def expert(place, blocks, w_first, w_second, sums, groups, relations, last):
    count = len(blocks)
    width, inner = w_first.shape
    slots = (blocks[0].shape[0] - EXTRA) * LANES // width
    rows = count * slots
    nodes = groups * relations * NODE_DEV
    if last:
        pieces = [jax.ShapeDtypeStruct((nodes // 16, width), BF16)] * 8
        shapes = pieces + [jax.ShapeDtypeStruct((rows, width), BF16), jax.ShapeDtypeStruct((nodes // 2, rows), BF16)]
    else:
        shapes = [jax.ShapeDtypeStruct((nodes, width), F32), jax.ShapeDtypeStruct((8, LANES), F32)]
    args = [place, *blocks, w_first, w_second] + ([] if sums is None else [sums])
    params = pltpu.CompilerParams(vmem_limit_bytes=(16 if relations <= 8 else 58) * MIB)
    outs = pl.pallas_call(
        functools.partial(expert_kernel, count, slots, groups, relations, sums is not None, last),
        out_shape=shapes,
        in_specs=[SM] + [VM] * (len(args) - 1),
        out_specs=[VM] * len(shapes),
        scratch_shapes=[
            pltpu.VMEM((rows, inner), BF16), pltpu.VMEM((nodes, rows), BF16), pltpu.VMEM((rows, width), BF16),
        ],
        compiler_params=params,
        cost_estimate=pl.CostEstimate(flops=1, bytes_accessed=1, transcendentals=0),
        name="expert",
    )(*args)
    if not last:
        return outs
    stay = pl.pallas_call(
        rest_kernel,
        out_shape=pieces,
        in_specs=[VM] * 3,
        out_specs=[VM] * 8,
        compiler_params=params,
        cost_estimate=pl.CostEstimate(flops=1, bytes_accessed=1, transcendentals=0),
        name="expert_rest",
    )(outs[8], outs[9], sums)
    return list(stay) + list(outs[:8])


def local(edge_feats, gain, w_in, w_out, rel_type, dst_node):
    rows = edge_feats.shape[1]
    width = edge_feats.shape[2]
    relations = lax.axis_size("rel")
    groups = lax.axis_size("dom")
    slots = 2 * rows // relations
    half = relations // 2
    mine = lax.axis_index("rel")
    place = jnp.stack([mine, lax.axis_index("dom") * relations + mine]).astype(I32)

    def move(value, dom_bits, rel_bits):
        pairs = [
            (r * groups + g, (r ^ rel_bits) * groups + (g ^ dom_bits))
            for r in range(relations) for g in range(groups)
        ]
        return lax.ppermute(value, ("rel", "dom"), pairs)

    step = half // 4
    far = [list(range(half + k * step, half + (k + 1) * step)) for k in range(4)]
    early, rest = far[0], list(range(half)) + far[1]
    first, kept = pack(
        place, rel_type.reshape(1, rows), dst_node, edge_feats[0], gain[None, :], relations, slots, early
    )
    held = {d: move(block, 0, d) for d, block in zip(early, first)}
    held.update({d: move(block, 0, d) if d else block for d, block in zip(rest, pack_more(kept, rest, slots))})

    def run(turn, sums, last=False):
        blocks = [held[d] for d in turn]
        return expert(place, blocks, w_in[0], w_out[0], sums, groups, relations, last)

    sums, token = run([0], None)
    for k in (2, 3):
        late = pack_more(kept, far[k], slots, [held[far[k - 2][-1]], token])
        held.update({d: move(block, 0, d) for d, block in zip(far[k], late)})
    for turn in (far[0] + [1], far[1] + list(range(2, half)), far[2]):
        sums, token = run(turn, sums)
    sums = run(far[3], sums, True)

    lines = sums[0].shape[0]
    away = {}
    for pair in PAIRS:
        got = move(jnp.concatenate([sums[8 + b] for b in pair]), 1, 0)
        away.update({b: got[i * lines : (i + 1) * lines] for i, b in enumerate(pair)})
    near = [sums[b].astype(F32) + away[b].astype(F32) for b in range(8)]
    total = near[0]
    for b in (7, 6, 5, 3, 4, 2, 1):
        total = total + move(near[b].astype(BF16), 2 * (b // 4), b // 2 % 2 + 2 * (b % 2)).astype(F32)
    total = total.reshape(relations // 4, NODE_DEV, -1)
    state = total[0]
    for f in range(relations // 4 - 1, 0, -1):
        state = state + move(total[f].astype(BF16), 0, 4 * f).astype(F32)
    return (state * (1.0 / math.sqrt(rows / NODE_DEV)))[None]


def solution(mesh):
    in_specs = (
        P("dom", "rel", None),
        P(),
        P("rel", None, None),
        P("rel", None, None),
        P("dom", "rel", None),
        P("dom", "rel"),
    )
    out_specs = P("dom", "rel", None)
    return jax.shard_map(local, mesh=mesh, in_specs=in_specs, out_specs=out_specs, check_vma=False)
```

```python
import functools
import math

import jax
import jax.numpy as jnp
from jax import lax
from jax.experimental import pallas as pl
from jax.experimental.pallas import tpu as pltpu
from jax.sharding import PartitionSpec as P

NODE_DEV = 32
LANES = 128
EXTRA = 16
PAIRS = ((1, 2), (4, 3, 5), (6, 7, 0))
MIB = 1024 * 1024
VM = pl.BlockSpec(memory_space=pltpu.VMEM)
SM = pl.BlockSpec(memory_space=pltpu.SMEM)
HB = pl.BlockSpec(memory_space=pltpu.HBM)
F32 = jnp.float32
BF16 = jnp.bfloat16
I32 = jnp.int32


def write_blocks(labels, slots, slot, coded, normed, blocks):
    rows, width = normed.shape
    for label, block in zip(labels, blocks):
        at = lax.broadcasted_iota(I32, (slots, rows), 0) + label * slots
        pick = (slot == at).astype(BF16)
        picked = jnp.dot(pick, normed, preferred_element_type=F32).astype(BF16)
        for c in range(width // LANES):
            block[c * slots : (c + 1) * slots, :] = picked[:, c * LANES : (c + 1) * LANES]
        ids = lax.dot_general(coded, pick, (((1,), (1,)), ((), ())), preferred_element_type=F32)
        block[width // LANES * slots :, :slots] = ids.astype(BF16)


def pack_kernel(relations, slots, labels, place_ref, kinds_hbm, dest_hbm, feats_hbm, gain_hbm, *refs):
    blocks, (normed_ref, slot_ref, coded_ref), scratch = (
        refs[: len(labels)], refs[len(labels) : -6], refs[-6:],
    )
    kinds_ref, dest_ref, gain_ref, feats_ref, sems, feat_sems = scratch
    rows, width = feats_ref.shape
    parts = 2
    part = rows // parts
    small = [
        pltpu.make_async_copy(kinds_hbm, kinds_ref, sems.at[0]),
        pltpu.make_async_copy(dest_hbm, dest_ref, sems.at[1]),
        pltpu.make_async_copy(gain_hbm, gain_ref, sems.at[2]),
    ]
    large = [
        pltpu.make_async_copy(
            feats_hbm.at[pl.ds(i * part, part), :], feats_ref.at[pl.ds(i * part, part), :], feat_sems.at[i]
        )
        for i in range(parts)
    ]
    for copy in small + large:
        copy.start()
    before = (
        lax.broadcasted_iota(I32, (rows, rows), 0) < lax.broadcasted_iota(I32, (rows, rows), 1)
    ).astype(BF16)
    for copy in small:
        copy.wait()
    offset = kinds_ref[...] ^ place_ref[0]
    marks = offset == lax.broadcasted_iota(I32, (max(relations, 16), rows), 0)
    count = jnp.dot(marks.astype(BF16), before, preferred_element_type=F32)
    rank = jnp.sum(jnp.where(marks, count, 0.0), axis=0, keepdims=True).astype(I32)
    slot = offset * slots + rank
    slot_ref[...] = slot
    dest = dest_ref[...]
    line = lax.broadcasted_iota(I32, (EXTRA, rows), 0)
    coded = jnp.where(
        line == 0, dest // NODE_DEV, jnp.where(line == 1, dest % NODE_DEV, jnp.where(line == 2, 1, 0))
    ).astype(BF16)
    coded_ref[...] = coded
    gain = gain_ref[...]
    for i in range(parts):
        large[i].wait()
        at = slice(i * part, (i + 1) * part)
        feats = feats_ref[at, :].astype(F32)
        scale = lax.rsqrt(jnp.mean(feats * feats, axis=1, keepdims=True) + 1e-06)
        normed_ref[at, :] = (feats * scale * gain).astype(BF16)
    write_blocks(labels, slots, slot, coded, normed_ref[...], blocks)


def pack_more_kernel(slots, labels, normed_ref, slot_ref, coded_ref, *refs):
    write_blocks(labels, slots, slot_ref[...], coded_ref[...], normed_ref[...], refs[-len(labels) :])


def pack_more(kept, labels, slots, after=()):
    rows, width = kept[0].shape
    block = jax.ShapeDtypeStruct((width // LANES * slots + EXTRA, LANES), BF16)
    return pl.pallas_call(
        functools.partial(pack_more_kernel, slots, labels),
        out_shape=[block] * len(labels),
        in_specs=[VM] * 3 + [HB] * len(after),
        out_specs=[VM] * len(labels),
        compiler_params=pltpu.CompilerParams(vmem_limit_bytes=16 * MIB),
        cost_estimate=pl.CostEstimate(flops=1, bytes_accessed=1, transcendentals=0),
        name="pack_more",
    )(*kept, *after)


def pack(place, kinds, dest, feats, gain, relations, slots, labels):
    rows, width = feats.shape
    block = jax.ShapeDtypeStruct((width // LANES * slots + EXTRA, LANES), BF16)
    shapes = [block] * len(labels) + [
        jax.ShapeDtypeStruct((rows, width), BF16),
        jax.ShapeDtypeStruct((1, rows), I32),
        jax.ShapeDtypeStruct((EXTRA, rows), BF16),
    ]
    outs = pl.pallas_call(
        functools.partial(pack_kernel, relations, slots, labels),
        out_shape=shapes,
        in_specs=[SM, HB, HB, HB, HB],
        out_specs=[VM] * len(shapes),
        scratch_shapes=[
            pltpu.VMEM((1, rows), I32),
            pltpu.VMEM((1, rows), I32),
            pltpu.VMEM((1, width), F32),
            pltpu.VMEM((rows, width), BF16),
            pltpu.SemaphoreType.DMA((3,)),
            pltpu.SemaphoreType.DMA((2,)),
        ],
        compiler_params=pltpu.CompilerParams(vmem_limit_bytes=16 * MIB),
        cost_estimate=pl.CostEstimate(flops=1, bytes_accessed=1, transcendentals=0),
        name="pack_far",
    )(place, *[pltpu.with_memory_space_constraint(a, pltpu.HBM) for a in (kinds, dest, feats, gain)])
    return outs[: len(labels)], outs[len(labels) :]


def gelu(x):
    return 0.5 * x * (1.0 + lax.erf(x * math.sqrt(0.5)))


def load_block(block_ref, x_ref, row, base, groups, relations):
    width = x_ref.shape[1]
    slots = (block_ref.shape[0] - EXTRA) * LANES // width
    for c in range(width // LANES):
        x_ref[row : row + slots, c * LANES : (c + 1) * LANES] = block_ref[c * slots : (c + 1) * slots, :]
    ids = block_ref[width // LANES * slots :, :slots].astype(F32).astype(I32)
    owner = ids[0:1] ^ base
    far = relations // 4
    y, z, f, g = owner % 2, owner // 2 % 2, owner // 4 % far, owner // relations
    at = (((((g % 2) * 2 + g // 2) * 2 + y) * 2 + z) * far + f) * NODE_DEV + ids[1:2]
    return jnp.where(ids[2:3] > 0, at, -1)


def up(x_ref, w_first_ref, hidden_ref):
    inner = w_first_ref.shape[1]
    part = 256

    def step(i, carry):
        at = pl.ds(pl.multiple_of(i * part, part), part)
        h = jnp.dot(x_ref[...], w_first_ref[:, at], preferred_element_type=F32)
        hidden_ref[:, at] = gelu(h).astype(BF16)
        return carry

    lax.fori_loop(0, inner // part, step, 0, unroll=8)


def down(hidden_ref, w_second_ref, table_ref, sums_ref, outs, kept):
    part = 256
    width = w_second_ref.shape[1]
    nodes = table_ref.shape[0]
    start = nodes // 2 if kept else 0
    messages = [
        jnp.dot(hidden_ref[...], w_second_ref[:, at : at + part], preferred_element_type=F32).astype(BF16)
        for at in range(0, width, part)
    ]
    for i, message in enumerate(messages):
        columns = slice(i * part, (i + 1) * part)
        if kept:
            kept[0][:, columns] = message
        add(table_ref[start:, :], message, sums_ref, start, columns, outs)
    if kept:
        kept[1][...] = table_ref[:start, :]


def add(table, message, sums_ref, start, columns, outs):
    total = jnp.dot(table, message, preferred_element_type=F32)
    piece = table.shape[0] // len(outs)
    if sums_ref is not None:
        total = total + sums_ref[start : start + table.shape[0], columns]
    for b, out in enumerate(outs):
        out[:, columns] = total[b * piece : (b + 1) * piece].astype(out.dtype)


def rest_kernel(messages_ref, table_ref, sums_ref, *outs):
    part = 256
    for at in range(0, messages_ref.shape[1], part):
        columns = slice(at, at + part)
        add(table_ref[...], messages_ref[:, columns], sums_ref, 0, columns, outs)


def expert_kernel(count, slots, groups, relations, has_sums, last, place_ref, *refs):
    blocks, refs = refs[:count], refs[count:]
    w_first_ref, w_second_ref, refs = refs[0], refs[1], refs[2:]
    sums_ref = None
    if has_sums:
        sums_ref, refs = refs[0], refs[1:]
    outs, (hidden_ref, table_ref, x_ref) = refs[:-3], refs[-3:]
    kept = ()
    if last:
        outs, kept = outs[:8], outs[8:]
    else:
        outs[-1][...] = jnp.zeros_like(outs[-1])
        outs = outs[:-1]
    nodes = table_ref.shape[0]
    for i in range(count):
        line = load_block(blocks[i], x_ref, i * slots, place_ref[1], groups, relations)
        table_ref[:, i * slots : (i + 1) * slots] = (
            line == lax.broadcasted_iota(I32, (nodes, slots), 0)
        ).astype(BF16)
    up(x_ref, w_first_ref, hidden_ref)
    down(hidden_ref, w_second_ref, table_ref, sums_ref, outs, kept)


def expert(place, blocks, w_first, w_second, sums, groups, relations, last):
    count = len(blocks)
    width, inner = w_first.shape
    slots = (blocks[0].shape[0] - EXTRA) * LANES // width
    rows = count * slots
    nodes = groups * relations * NODE_DEV
    if last:
        pieces = [jax.ShapeDtypeStruct((nodes // 16, width), BF16)] * 8
        shapes = pieces + [jax.ShapeDtypeStruct((rows, width), BF16), jax.ShapeDtypeStruct((nodes // 2, rows), BF16)]
    else:
        shapes = [jax.ShapeDtypeStruct((nodes, width), F32), jax.ShapeDtypeStruct((8, LANES), F32)]
    args = [place, *blocks, w_first, w_second] + ([] if sums is None else [sums])
    params = pltpu.CompilerParams(vmem_limit_bytes=(16 if relations <= 8 else 58) * MIB)
    outs = pl.pallas_call(
        functools.partial(expert_kernel, count, slots, groups, relations, sums is not None, last),
        out_shape=shapes,
        in_specs=[SM] + [VM] * (len(args) - 1),
        out_specs=[VM] * len(shapes),
        scratch_shapes=[
            pltpu.VMEM((rows, inner), BF16), pltpu.VMEM((nodes, rows), BF16), pltpu.VMEM((rows, width), BF16),
        ],
        compiler_params=params,
        cost_estimate=pl.CostEstimate(flops=1, bytes_accessed=1, transcendentals=0),
        name="expert",
    )(*args)
    if not last:
        return outs
    stay = pl.pallas_call(
        rest_kernel,
        out_shape=pieces,
        in_specs=[VM] * 3,
        out_specs=[VM] * 8,
        compiler_params=params,
        cost_estimate=pl.CostEstimate(flops=1, bytes_accessed=1, transcendentals=0),
        name="expert_rest",
    )(outs[8], outs[9], sums)
    return list(stay) + list(outs[:8])


def local(edge_feats, gain, w_in, w_out, rel_type, dst_node):
    rows = edge_feats.shape[1]
    width = edge_feats.shape[2]
    relations = lax.axis_size("rel")
    groups = lax.axis_size("dom")
    slots = 2 * rows // relations
    half = relations // 2
    mine = lax.axis_index("rel")
    place = jnp.stack([mine, lax.axis_index("dom") * relations + mine]).astype(I32)

    def move(value, dom_bits, rel_bits):
        pairs = [
            (r * groups + g, (r ^ rel_bits) * groups + (g ^ dom_bits))
            for r in range(relations) for g in range(groups)
        ]
        return lax.ppermute(value, ("rel", "dom"), pairs)

    step = half // 4
    far = [list(range(half + k * step, half + (k + 1) * step)) for k in range(4)]
    early, rest = far[0], list(range(half)) + far[1]
    first, kept = pack(
        place, rel_type.reshape(1, rows), dst_node, edge_feats[0], gain[None, :], relations, slots, early
    )
    held = {d: move(block, 0, d) for d, block in zip(early, first)}
    held.update({d: move(block, 0, d) if d else block for d, block in zip(rest, pack_more(kept, rest, slots))})

    def run(turn, sums, last=False):
        blocks = [held[d] for d in turn]
        return expert(place, blocks, w_in[0], w_out[0], sums, groups, relations, last)

    sums, token = run([0], None)
    for k in (2, 3):
        late = pack_more(kept, far[k], slots, [held[far[k - 2][-1]], token])
        held.update({d: move(block, 0, d) for d, block in zip(far[k], late)})
    for turn in (far[0] + [1], far[1] + list(range(2, half)), far[2]):
        sums, token = run(turn, sums)
    sums = run(far[3], sums, True)

    lines = sums[0].shape[0]
    away = {}
    for pair in PAIRS:
        got = move(jnp.concatenate([sums[8 + b] for b in pair]), 1, 0)
        away.update({b: got[i * lines : (i + 1) * lines] for i, b in enumerate(pair)})
    near = [sums[b].astype(F32) + away[b].astype(F32) for b in range(8)]
    total = near[0]
    for b in (7, 6, 5, 3, 4, 2, 1):
        total = total + move(near[b].astype(BF16), 2 * (b // 4), b // 2 % 2 + 2 * (b % 2)).astype(F32)
    total = total.reshape(relations // 4, NODE_DEV, -1)
    state = total[0]
    for f in range(relations // 4 - 1, 0, -1):
        state = state + move(total[f].astype(BF16), 0, 4 * f).astype(F32)
    return (state * (1.0 / math.sqrt(rows / NODE_DEV)))[None]


def solution(mesh):
    in_specs = (
        P("dom", "rel", None),
        P(),
        P("rel", None, None),
        P("rel", None, None),
        P("dom", "rel", None),
        P("dom", "rel"),
    )
    out_specs = P("dom", "rel", None)
    return jax.shard_map(local, mesh=mesh, in_specs=in_specs, out_specs=out_specs, check_vma=False)
```
